512 devices in a mesh: freq: 16 (over z_lo, x), layer: 32 (over z_hi, y, core).
Axes of the slice: x: 4, y: 8, z: 8 (z_hi: 2, z_lo: 4; z = z_hi * 4 + z_lo), core: 2. Of those that a mesh axis runs over, the one named last changes fastest.
Arguments:
- conductivity: float32 [32, 128, 128], P('layer'), may hold values from 0.1 to 1
- background: float32 [16, 2, 2, 32, 128, 128], P('freq', None, None, 'layer'), may hold values from -6 to 6
- green: float32 [16, 2, 32, 256, 256], P('freq', None, None, 'layer'), may hold values from -2 to 2
- pair_table: int32 [32, 32], replicated, may hold values from 0 to 31, as said below
- stations: int32 [32, 128], P('layer'), may hold values from 0 to 16383, as said below
- observed: float32 [16, 2, 2, 32, 128], P('freq', None, None, 'layer'), may hold values from -6 to 6
- data_error: float32 [16, 2, 32, 128], P('freq', None, 'layer'), may hold values from 0.3 to 3
Outputs:
- gradient: float32 [32, 128, 128], P('layer')
The draws below stay inside these ranges and needn't reach their ends.
Inputs may be any that keep to these rules, and one draw needn't show every extreme that they name: pair_table[i, j] == pair_table[j, i]. row-major cell index x * 128 + y within the station's layer; stations may share a cell.
All inputs are finite; a program needn't handle non-finite values.
Results may differ from the reference program's by a relative error of at most 0.000073.
Values sent between devices are 32-bit elements; how exact they have to be, the bound alone decides.
No kernel may reach another device: no remote copies, remote signals or barrier semaphores. Data moves between devices by JAX's collectives and lax.ppermute only.
A program may use at most 64 MiB of HBM per device.

```python
import math
import jax
import jax.numpy as jnp
from jax import lax

NX = 128
NY = 128
POLS = 2
STA_LAY = 128
KX = 256
KY = 256
LAYERS = 32
NSPEC = 32
FREQS = 16


def draw_pair_table(key, part):
    key = jax.random.fold_in(key, 11)
    base_draw = jax.random.randint(key, (LAYERS, LAYERS), 0, NSPEC, dtype=jnp.int32)
    upper_mask = jnp.arange(LAYERS)[:, None] <= jnp.arange(LAYERS)[None, :]
    pair_ids = jnp.where(upper_mask, base_draw, base_draw.T)
    pair_ids = pair_ids.at[0, LAYERS - 1].set(NSPEC - 1).at[LAYERS - 1, 0].set(NSPEC - 1)
    return pair_ids.at[0, 0].set(0)


def draw_stations(key, part):
    key = jax.random.fold_in(key, 23)
    cell_ids = jax.random.randint(key, (LAYERS, STA_LAY), 0, NX * NY, dtype=jnp.int32)
    cell_ids = cell_ids.at[0, 0].set(0)
    return cell_ids.at[LAYERS - 1, STA_LAY - 1].set(NX * NY - 1)


def levels(key, extent, cuts, least, largest):
    def one(position, parts):
        steps = jax.random.uniform(jax.random.fold_in(jax.random.fold_in(key, 6), position), (parts,), jnp.float32, least / len(cuts), largest / len(cuts))
        return jnp.repeat(jnp.exp(steps), extent[position] // parts).reshape((-1,) + (1,) * (len(extent) - position - 1))

    level = one(*cuts[0])
    for cut in cuts[1:]:
        level = level * one(*cut)
    return level


def centred(own_key, dims, spread, limit, cuts=(), kind=jnp.bfloat16):
    gain = levels(own_key, dims, cuts, -0.22, 0.18) if cuts else 1.0
    values = jax.random.normal(own_key, dims, jnp.float32) * spread * gain
    return jnp.minimum(jnp.maximum(values, -limit), limit).astype(kind)


def setup_inputs(seed: int = 0) -> dict:
    key_of = jax.random.split(jax.random.key(seed), 8)
    return {
        "conductivity": jnp.clip(jnp.exp(math.log(1.0) - 2.3025851 * jax.random.uniform(key_of[0], (LAYERS, NX, NY), jnp.float32) ** levels(key_of[0], (LAYERS, NX, NY), ((0, 32),), -0.2, 0.2)), 0.1, 1.0),
        "background": centred(key_of[1], (FREQS, POLS, 2, LAYERS, NX, NY), 1.0, 6.0, ((0, 16), (3, 32)), jnp.float32),
        "green": centred(key_of[2], (FREQS, 2, NSPEC, KX, KY), 0.15, 2.0, ((0, 16), (3, 32)), jnp.float32),
        "pair_table": draw_pair_table(jax.random.fold_in(key_of[7], 71), 0),
        "stations": draw_stations(jax.random.fold_in(key_of[7], 71), 0),
        "observed": centred(key_of[5], (FREQS, POLS, 2, LAYERS, STA_LAY), 1.0, 6.0, ((0, 16), (3, 32)), jnp.float32),
        "data_error": jnp.clip(jnp.exp(math.log(3.0) - 2.3025851 * jax.random.uniform(key_of[6], (FREQS, POLS, LAYERS, STA_LAY), jnp.float32) ** levels(key_of[6], (FREQS, POLS, LAYERS, STA_LAY), ((0, 16), (2, 32)), -0.2, 0.2)), 0.3, 3.0),
    }


HIGHEST = lax.Precision.HIGHEST


def dft_tables(wave_count, cell_count):
    wave_ids = jnp.arange(wave_count, dtype=jnp.int32)[:, None]
    cell_ids = jnp.arange(cell_count, dtype=jnp.int32)[None, :]
    phases = (wave_ids * cell_ids) % wave_count
    angles = phases.astype(jnp.float32) * (2.0 * math.pi / wave_count)
    return jnp.cos(angles), jnp.sin(angles)


def forward_rows(re_part, im_part, cosine_table, sine_table):
    cos_re = jnp.einsum("kx,...xy->...ky", cosine_table, re_part, precision=HIGHEST)
    cos_im = jnp.einsum("kx,...xy->...ky", cosine_table, im_part, precision=HIGHEST)
    sin_re = jnp.einsum("kx,...xy->...ky", sine_table, re_part, precision=HIGHEST)
    sin_im = jnp.einsum("kx,...xy->...ky", sine_table, im_part, precision=HIGHEST)
    return cos_re + sin_im, cos_im - sin_re


def forward_cols(re_part, im_part, cosine_table, sine_table):
    cos_re = jnp.einsum("...y,ky->...k", re_part, cosine_table, precision=HIGHEST)
    cos_im = jnp.einsum("...y,ky->...k", im_part, cosine_table, precision=HIGHEST)
    sin_re = jnp.einsum("...y,ky->...k", re_part, sine_table, precision=HIGHEST)
    sin_im = jnp.einsum("...y,ky->...k", im_part, sine_table, precision=HIGHEST)
    return cos_re + sin_im, cos_im - sin_re


def inverse_cols(re_part, im_part, cosine_table, sine_table):
    scale = 1.0 / cosine_table.shape[0]
    cos_re = jnp.einsum("...k,ky->...y", re_part, cosine_table, precision=HIGHEST)
    cos_im = jnp.einsum("...k,ky->...y", im_part, cosine_table, precision=HIGHEST)
    sin_re = jnp.einsum("...k,ky->...y", re_part, sine_table, precision=HIGHEST)
    sin_im = jnp.einsum("...k,ky->...y", im_part, sine_table, precision=HIGHEST)
    return (cos_re - sin_im) * scale, (cos_im + sin_re) * scale


def inverse_rows(re_part, im_part, cosine_table, sine_table):
    scale = 1.0 / cosine_table.shape[0]
    cos_re = jnp.einsum("kx,...ky->...xy", cosine_table, re_part, precision=HIGHEST)
    cos_im = jnp.einsum("kx,...ky->...xy", cosine_table, im_part, precision=HIGHEST)
    sin_re = jnp.einsum("kx,...ky->...xy", sine_table, re_part, precision=HIGHEST)
    sin_im = jnp.einsum("kx,...ky->...xy", sine_table, im_part, precision=HIGHEST)
    return (cos_re - sin_im) * scale, (cos_im + sin_re) * scale


def mix_layers(spec_real, spec_imag, green_real, green_imag, pair_table):
    def one_receiver(table_row):
        row_real = jnp.take(green_real, table_row, axis=0)
        row_imag = jnp.take(green_imag, table_row, axis=0)
        out_real = jnp.sum(row_real * spec_real - row_imag * spec_imag, axis=1)
        out_imag = jnp.sum(row_real * spec_imag + row_imag * spec_real, axis=1)
        return out_real, out_imag

    mixed_real, mixed_imag = lax.map(one_receiver, pair_table)
    return jnp.moveaxis(mixed_real, 0, 1), jnp.moveaxis(mixed_imag, 0, 1)


def apply_green(src_real, src_imag, green_real, green_imag, pair_table):
    cosine_x, sine_x = dft_tables(KX, NX)
    cosine_y, sine_y = dft_tables(KY, NY)
    rows_real, rows_imag = forward_rows(src_real, src_imag, cosine_x, sine_x)
    spec_real, spec_imag = forward_cols(rows_real, rows_imag, cosine_y, sine_y)
    mixed_real, mixed_imag = mix_layers(spec_real, spec_imag, green_real, green_imag, pair_table)
    cols_real, cols_imag = inverse_cols(mixed_real, mixed_imag, cosine_y, sine_y)
    return inverse_rows(cols_real, cols_imag, cosine_x, sine_x)


def station_residual(total_real, total_imag, stations, measured, errors):
    pol_count = total_real.shape[0]
    layer_count = total_real.shape[1]
    flat_real = total_real.reshape(pol_count, layer_count, -1)
    flat_imag = total_imag.reshape(pol_count, layer_count, -1)
    station_idx = jnp.broadcast_to(stations[None], (pol_count,) + stations.shape)
    pred_real = jnp.take_along_axis(flat_real, station_idx, axis=2)
    pred_imag = jnp.take_along_axis(flat_imag, station_idx, axis=2)
    weight = errors * errors
    resid_real = (pred_real - measured[:, 0]) / weight
    resid_imag = (pred_imag - measured[:, 1]) / weight
    layer_ids = jnp.arange(layer_count, dtype=jnp.int32)[:, None]
    source_real = jnp.zeros_like(flat_real).at[:, layer_ids, stations].add(resid_real)
    source_imag = jnp.zeros_like(flat_imag).at[:, layer_ids, stations].add(-resid_imag)
    return source_real.reshape(total_real.shape), source_imag.reshape(total_imag.shape)


def reference(conductivity, background, green, pair_table, stations, observed, data_error):
    def one_frequency(inputs):
        field_pair, spectra, measured, errors = inputs
        bg_real = field_pair[:, 0]
        bg_imag = field_pair[:, 1]
        scat_real, scat_imag = apply_green(conductivity * bg_real, conductivity * bg_imag, spectra[0], spectra[1], pair_table)
        total_real = bg_real + scat_real
        total_imag = bg_imag + scat_imag
        source_real, source_imag = station_residual(total_real, total_imag, stations, measured, errors)
        adj_real, adj_imag = apply_green(source_real, source_imag, spectra[0], spectra[1], pair_table)
        return jnp.sum(total_real * adj_real - total_imag * adj_imag, axis=0)

    freq_terms = lax.map(one_frequency, (background, green, observed, data_error))
    return jnp.sum(freq_terms, axis=0)
```

```python
import functools
import math

import jax
import jax.numpy as jnp
import ml_dtypes
import numpy as np
from jax import lax
from jax.experimental import pallas as pl
from jax.experimental.pallas import tpu as pltpu
from jax.sharding import PartitionSpec as P

CELLS = 128
WAVES = 256
LAYERS = 32
ROWS = 8
POLS = 2
GROUP = 4
STEP = 8
RING = 4
F32 = jnp.float32
BF16 = jnp.bfloat16
VMEM_BYTES = 40 * 1024 * 1024


def halves(table):
    high = table.astype(ml_dtypes.bfloat16)
    low = (table - high.astype(np.float64)).astype(ml_dtypes.bfloat16)
    return high, low


def dft_blocks():
    waves = np.arange(WAVES)[:, None]
    cells = np.arange(CELLS)[None, :]
    angles = (waves * cells % WAVES) * (2.0 * math.pi / WAVES)
    cos, sin = np.cos(angles), np.sin(angles)
    x_fwd = np.block([[cos, sin], [-sin, cos]])
    y_fwd = np.block([[cos.T, -sin.T], [sin.T, cos.T]])
    y_inv = np.block([[cos, sin], [-sin, cos]]) / WAVES
    x_inv = np.block([[cos.T, -sin.T], [sin.T, cos.T]]) / WAVES
    return x_fwd, y_fwd, y_inv, x_inv


def left_table(table):
    high, low = halves(table)
    return np.concatenate([high, high, low], axis=1)


def right_table(table):
    high, low = halves(table)
    return np.concatenate([high, high, low], axis=0)


def split_cat(values, axis):
    high = values.astype(BF16)
    low = (values - high.astype(F32)).astype(BF16)
    return jnp.concatenate([high, low, high], axis=axis)


def x_forward_kernel(cond_ref, field_ref, table_ref, out_ref):
    cond = cond_ref[0]
    parts = [
        jnp.concatenate([cond * field_ref[0, p, c, 0] for p in range(POLS)], axis=1)
        for c in range(2)
    ]
    cells = jnp.concatenate(parts, axis=0)
    rows = jnp.dot(table_ref[...], split_cat(cells, 0), preferred_element_type=F32)
    for p in range(POLS):
        for c in range(2):
            block = rows[c * WAVES : (c + 1) * WAVES, p * CELLS : (p + 1) * CELLS]
            out_ref[:, 2 * p + c] = block.reshape(LAYERS, ROWS, CELLS)


def mix_rows(rows_ref, green_ref, pair_ref, fwd_ref, inv_ref, out_ref, spec_ref, kern_ref, mixed_ref):
    for h in range(2):
        lanes = slice(h * CELLS, (h + 1) * CELLS)
        g_re = green_ref[0, 0, :, :, lanes]
        g_im = green_ref[0, 1, :, :, lanes]
        kern_ref[h, :, 0] = g_re + g_im
        kern_ref[h, :, 1] = g_re
        kern_ref[h, :, 2] = g_im
    for p in range(POLS):
        flat = [rows_ref[:, 2 * p + c].reshape(LAYERS * ROWS, CELLS) for c in range(2)]
        both = jnp.concatenate(flat, axis=1)
        spec = jnp.dot(split_cat(both, 1), fwd_ref[...], preferred_element_type=F32)
        for h in range(2):
            re = spec[:, h * CELLS : (h + 1) * CELLS].reshape(LAYERS, ROWS, CELLS)
            im = spec[:, WAVES + h * CELLS : WAVES + (h + 1) * CELLS].reshape(LAYERS, ROWS, CELLS)
            spec_ref[h, :, 3 * p] = re
            spec_ref[h, :, 3 * p + 1] = im - re
            spec_ref[h, :, 3 * p + 2] = re + im

    for h in range(2):

        def one_group(group, carry, h=h):
            first = group * GROUP

            def some_sources(chunk, sums):
                sums = list(sums)
                for s in range(STEP):
                    j = chunk * STEP + s
                    src = [spec_ref[h, j, k] for k in range(3 * POLS)]
                    for r in range(GROUP):
                        n = pair_ref[first + r, j]
                        kern = [kern_ref[h, n, k] for k in range(3)]
                        for p in range(POLS):
                            for k in range(3):
                                at = (r * POLS + p) * 3 + k
                                sums[at] = sums[at] + kern[k] * src[3 * p + k]
                return tuple(sums)

            zero = jnp.zeros((ROWS, CELLS), F32)
            sums = lax.fori_loop(
                0, LAYERS // STEP, some_sources, (zero,) * (GROUP * POLS * 3)
            )
            for r in range(GROUP):
                for p in range(POLS):
                    one, two, three = sums[(r * POLS + p) * 3 : (r * POLS + p) * 3 + 3]
                    mixed_ref[p, first + r, :, h * CELLS : (h + 1) * CELLS] = one - three
                    mixed_ref[p, first + r, :, WAVES + h * CELLS : WAVES + (h + 1) * CELLS] = one + two
            return carry

        lax.fori_loop(0, LAYERS // GROUP, one_group, 0)

    for p in range(POLS):
        mixed = mixed_ref[p].reshape(LAYERS * ROWS, 2 * WAVES)
        back = jnp.dot(split_cat(mixed, 1), inv_ref[...], preferred_element_type=F32)
        for c in range(2):
            out_ref[:, 2 * p + c] = back[:, c * CELLS : (c + 1) * CELLS].reshape(LAYERS, ROWS, CELLS)


def mix_kernel(pair_ref, rows_ref, green_ref, fwd_ref, inv_ref, out_ref, spec_ref, kern_ref, mixed_ref):
    mix_rows(rows_ref, green_ref, pair_ref, fwd_ref, inv_ref, out_ref, spec_ref, kern_ref, mixed_ref)


def sin_pi(v):
    square = v * v
    total = jnp.full_like(v, math.pi**13 / math.factorial(13))
    for order in (11, 9, 7, 5, 3, 1):
        sign = -1.0 if (order // 2) % 2 else 1.0
        total = total * square + sign * math.pi**order / math.factorial(order)
    return total * v


def adjoint_mix_kernel(
    pair_ref, first_ref, sent_ref, green_ref, fwd_ref, inv_ref,
    out_ref, rows_ref, spec_ref, kern_ref, mixed_ref,
):
    cell = sent_ref[:, 4:5, :].astype(jnp.int32)
    x_cell = cell >> 7
    wave = first_ref[0] + lax.broadcasted_iota(jnp.int32, (LAYERS, ROWS, CELLS), 1)
    turn = (wave * x_cell) & (WAVES - 1)
    u = (turn.astype(F32) - WAVES / 2) * (2.0 / WAVES)
    size = jnp.abs(u)
    cos = -sin_pi(0.5 - size)
    sin = sin_pi(jnp.minimum(size, 1.0 - size))
    sin = jnp.where(u < 0, sin, -sin)
    for p in range(POLS):
        re = sent_ref[:, 2 * p : 2 * p + 1, :]
        im = sent_ref[:, 2 * p + 1 : 2 * p + 2, :]
        rows_ref[:, 2 * p] = re * cos + im * sin
        rows_ref[:, 2 * p + 1] = im * cos - re * sin
    y_ids = lax.broadcasted_iota(jnp.int32, (CELLS, CELLS), 0)
    for j in range(LAYERS):
        y_cell = cell[j] & (CELLS - 1)
        spot = jnp.where(y_ids == y_cell, 1.0, 0.0).astype(BF16)
        values = rows_ref[j].reshape(4 * ROWS, CELLS)
        high = values.astype(BF16)
        low = (values - high.astype(F32)).astype(BF16)
        at_y = lax.dot_general(
            jnp.concatenate([high, low], axis=0), spot, (((1,), (1,)), ((), ())),
            preferred_element_type=F32,
        )
        rows_ref[j] = (at_y[: 4 * ROWS] + at_y[4 * ROWS :]).reshape(4, ROWS, CELLS)
    mix_rows(rows_ref, green_ref, pair_ref, fwd_ref, inv_ref, out_ref, spec_ref, kern_ref, mixed_ref)


def x_inverse(rows_ref, table_ref):
    parts = [
        jnp.concatenate(
            [rows_ref[:, 2 * p + c].reshape(WAVES, CELLS) for p in range(POLS)], axis=1
        )
        for c in range(2)
    ]
    waves = jnp.concatenate(parts, axis=0)
    cells = jnp.dot(table_ref[...], split_cat(waves, 0), preferred_element_type=F32)
    return [
        [cells[c * CELLS : (c + 1) * CELLS, p * CELLS : (p + 1) * CELLS] for c in range(2)]
        for p in range(POLS)
    ]


def residual_kernel(rows_ref, field_ref, station_ref, seen_ref, error_ref, table_ref, total_ref, sent_ref):
    scattered = x_inverse(rows_ref, table_ref)
    cell = station_ref[...]
    ids = lax.broadcasted_iota(jnp.int32, (CELLS, CELLS), 0)
    x_spot = jnp.where(ids == (cell >> 7), 1.0, 0.0).astype(BF16)
    y_spot = ids == (cell & (CELLS - 1))
    sent = []
    for p in range(POLS):
        weight = error_ref[0, p] * error_ref[0, p]
        for c in range(2):
            total = field_ref[0, p, c, 0] + scattered[p][c]
            total_ref[2 * p + c] = total
            turned = total.T
            picked = jnp.zeros((CELLS, CELLS), F32)
            for _ in range(3):
                piece = turned.astype(BF16)
                picked = picked + jnp.dot(piece, x_spot, preferred_element_type=F32)
                turned = turned - piece.astype(F32)
            predicted = jnp.sum(jnp.where(y_spot, picked, 0.0), axis=0, keepdims=True)
            resid = (predicted - seen_ref[0, p, c]) / weight
            sent.append(-resid if c else resid)
    sent.append(cell.astype(F32))
    sent.append(jnp.zeros((3, CELLS), F32))
    message = jnp.concatenate(sent, axis=0)
    sent_ref[...] = jnp.broadcast_to(message[None], (LAYERS, 8, CELLS))


def gradient_kernel(rows_ref, total_ref, table_ref, out_ref):
    adjoint = x_inverse(rows_ref, table_ref)
    term = jnp.zeros((CELLS, CELLS), F32)
    for p in range(POLS):
        term = term + (total_ref[2 * p] * adjoint[p][0] - total_ref[2 * p + 1] * adjoint[p][1])
    out_ref[...] = jnp.broadcast_to(term[None], (RING, CELLS, CELLS))


def call(kernel, out_shape, scratch=(), smem=0, operands=()):
    specs = [pl.BlockSpec(memory_space=pltpu.SMEM)] * smem
    specs += [pl.BlockSpec(memory_space=pltpu.VMEM)] * (len(operands) - smem)
    if isinstance(out_shape, list):
        out_specs = [pl.BlockSpec(memory_space=pltpu.VMEM)] * len(out_shape)
    else:
        out_specs = pl.BlockSpec(memory_space=pltpu.VMEM)
    return pl.pallas_call(
        kernel,
        out_shape=out_shape,
        in_specs=specs,
        out_specs=out_specs,
        scratch_shapes=list(scratch),
        compiler_params=pltpu.CompilerParams(vmem_limit_bytes=VMEM_BYTES),
    )(*operands)


def over_layers(values):
    return lax.all_to_all(values, "layer", split_axis=0, concat_axis=0, tiled=True)


def sum_over_freq(copies, size):
    rings = [list(range(r, r + RING)) for r in range(0, size, RING)]
    lines = [list(range(r, size, RING)) for r in range(RING)]
    for groups in (rings, lines):
        parts = lax.all_to_all(
            copies, "freq", split_axis=0, concat_axis=0, tiled=True, axis_index_groups=groups
        )
        total = (parts[0] + parts[1]) + (parts[2] + parts[3])
        copies = jnp.broadcast_to(total[None], copies.shape)
    return total


def per_device(conductivity, background, green, pair_table, stations, observed, data_error, freqs):
    x_fwd, y_fwd, y_inv, x_inv = dft_blocks()
    x_fwd, x_inv = left_table(x_fwd), left_table(x_inv)
    y_fwd, y_inv = right_table(y_fwd), right_table(y_inv)
    rows_shape = jax.ShapeDtypeStruct((LAYERS, 4, ROWS, CELLS), F32)
    scratch = (
        pltpu.VMEM((2, LAYERS, 3 * POLS, ROWS, CELLS), F32),
        pltpu.VMEM((2, green.shape[2], 3, ROWS, CELLS), F32),
        pltpu.VMEM((POLS, LAYERS, ROWS, 2 * WAVES), F32),
    )
    rows = call(x_forward_kernel, rows_shape, operands=(conductivity, background, x_fwd))
    back = call(
        mix_kernel, rows_shape, scratch, 1,
        (pair_table, over_layers(rows), green, y_fwd, y_inv),
    )
    total, sent = call(
        residual_kernel,
        [
            jax.ShapeDtypeStruct((4, CELLS, CELLS), F32),
            jax.ShapeDtypeStruct((LAYERS, 8, CELLS), F32),
        ],
        operands=(over_layers(back), background, stations, observed, data_error, x_inv),
    )
    first = (lax.axis_index("layer") * ROWS).astype(jnp.int32).reshape(1)
    back = call(
        adjoint_mix_kernel, rows_shape,
        (pltpu.VMEM((LAYERS, 4, ROWS, CELLS), F32),) + scratch, 2,
        (pair_table, first, over_layers(sent), green, y_fwd, y_inv),
    )
    copies = call(
        gradient_kernel,
        jax.ShapeDtypeStruct((RING, CELLS, CELLS), F32),
        operands=(over_layers(back), total, x_inv),
    )
    return sum_over_freq(copies, freqs)[None]


def solution(mesh):
    in_specs = (
        P("layer", None, None),
        P("freq", None, None, "layer", None, None),
        P("freq", None, None, "layer", None),
        P(),
        P("layer", None),
        P("freq", None, None, "layer", None),
        P("freq", None, "layer", None),
    )
    return jax.shard_map(
        functools.partial(per_device, freqs=mesh.shape["freq"]),
        mesh=mesh, in_specs=in_specs, out_specs=P("layer", None, None), check_vma=False,
    )
```

```python
import functools
import math

import jax
import jax.numpy as jnp
import ml_dtypes
import numpy as np
from jax import lax
from jax.experimental import pallas as pl
from jax.experimental.pallas import tpu as pltpu
from jax.sharding import PartitionSpec as P

CELLS = 128
WAVES = 256
LAYERS = 32
ROWS = 8
KERNELS = 32
POLS = 2
GROUP = 4
STEP = 16
RING = 4
F32 = jnp.float32
BF16 = jnp.bfloat16
VMEM_BYTES = 40 * 1024 * 1024
FIRST_BYTES = 60 * 1024 * 1024


def halves(table):
    high = table.astype(ml_dtypes.bfloat16)
    low = (table - high.astype(np.float64)).astype(ml_dtypes.bfloat16)
    return high, low


def dft_blocks():
    waves = np.arange(WAVES)[:, None]
    cells = np.arange(CELLS)[None, :]
    angles = (waves * cells % WAVES) * (2.0 * math.pi / WAVES)
    cos, sin = np.cos(angles), np.sin(angles)
    x_fwd = np.concatenate(halves(np.concatenate([cos, sin], axis=1)), axis=1)
    y_fwd = np.block([[cos.T, -sin.T], [sin.T, cos.T]])
    y_inv = np.block([[cos, sin], [-sin, cos]]) / WAVES
    x_inv = np.block([[cos.T, -sin.T], [sin.T, cos.T]]) / WAVES
    return x_fwd, y_fwd, y_inv, x_inv


def left_table(table):
    high, low = halves(table)
    return np.concatenate([high, high, low], axis=1)


def right_table(table):
    high, low = halves(table)
    return np.concatenate([high, high, low], axis=0)


def split_cat(values, axis):
    high = values.astype(BF16)
    low = (values - high.astype(F32)).astype(BF16)
    return jnp.concatenate([high, low, high], axis=axis)


def x_forward_kernel(cond_hbm, field_hbm, table_hbm, out_ref, cond_ref, field_ref, table_ref, sems):
    copies = [
        pltpu.make_async_copy(source, target, sems.at[n])
        for n, (source, target) in enumerate(
            ((field_hbm, field_ref), (cond_hbm, cond_ref), (table_hbm, table_ref))
        )
    ]
    for copy in copies:
        copy.start()
    copies[0].wait()
    copies[1].wait()
    cond = cond_ref[0]
    high, low = [], []
    for c in range(2):
        part = jnp.concatenate([cond * field_ref[0, p, c, 0] for p in range(POLS)], axis=1)
        high.append(part.astype(BF16))
        low.append((part - high[c].astype(F32)).astype(BF16))
    stacks = [
        jnp.concatenate([jnp.concatenate([part[0], part[1]], axis=1), jnp.concatenate([part[1], -part[0]], axis=1)], axis=0)
        for part in (high, low)
    ]
    cells = jnp.concatenate([stacks[0], stacks[1], stacks[0]], axis=0)
    copies[2].wait()
    table = table_ref[...]
    table = jnp.concatenate([table[:, :WAVES], table], axis=1)
    rows = jnp.dot(table, cells, preferred_element_type=F32)
    for c in range(2):
        for p in range(POLS):
            at = (c * POLS + p) * CELLS
            out_ref[:, 2 * p + c] = rows[:, at : at + CELLS].reshape(LAYERS, ROWS, CELLS)


def mix_rows(rows_ref, green_ref, place_ref, fwd_ref, inv_ref, out_ref, spec_ref, kern_ref, mixed_ref):
    lanes = [slice(h * CELLS, (h + 1) * CELLS) for h in range(2)]
    for h in range(2):
        g_re = green_ref[0, 0, :, :, lanes[h]]
        g_im = green_ref[0, 1, :, :, lanes[h]]
        kern_ref[h, :, 0:ROWS] = g_re + g_im
        kern_ref[h, :, ROWS : 2 * ROWS] = g_re
        kern_ref[h, :, 2 * ROWS :] = g_im
    for p in range(POLS):
        flat = [rows_ref[:, 2 * p + c].reshape(LAYERS * ROWS, CELLS) for c in range(2)]
        both = jnp.concatenate(flat, axis=1)
        spec = jnp.dot(split_cat(both, 1), fwd_ref[...], preferred_element_type=F32)
        for h in range(2):
            re = spec[:, h * CELLS : (h + 1) * CELLS].reshape(LAYERS, ROWS, CELLS)
            im = spec[:, WAVES + h * CELLS : WAVES + (h + 1) * CELLS].reshape(LAYERS, ROWS, CELLS)
            for k, value in enumerate((re, im - re, re + im)):
                at = (3 * p + k) * ROWS
                spec_ref[h, :, at : at + ROWS] = value

    kern = [kern_ref.at[h].reshape(KERNELS * 3 * ROWS, CELLS) for h in range(2)]
    for h in range(2):

        def one_group(group, carry, h=h):
            first = group * GROUP

            def some_sources(chunk, sums):
                sums = list(sums)
                base = first * LAYERS + chunk * STEP
                for s in range(STEP):
                    j = chunk * STEP + s
                    src = [spec_ref[h, j, k * ROWS : (k + 1) * ROWS] for k in range(3 * POLS)]
                    for r in range(GROUP):
                        place = place_ref[base + (r * LAYERS + s)]
                        for k in range(3):
                            row = pl.multiple_of(place + k * ROWS, ROWS)
                            factor = kern[h][pl.ds(row, ROWS), :]
                            for p in range(POLS):
                                at = (r * POLS + p) * 3 + k
                                sums[at] = sums[at] + factor * src[3 * p + k]
                return tuple(sums)

            zero = jnp.zeros((ROWS, CELLS), F32)
            sums = lax.fori_loop(
                0, LAYERS // STEP, some_sources, (zero,) * (GROUP * POLS * 3)
            )
            for r in range(GROUP):
                for p in range(POLS):
                    one, two, three = sums[(r * POLS + p) * 3 : (r * POLS + p) * 3 + 3]
                    mixed_ref[p, first + r, :, h * CELLS : (h + 1) * CELLS] = one - three
                    mixed_ref[p, first + r, :, WAVES + h * CELLS : WAVES + (h + 1) * CELLS] = one + two
            return carry

        lax.fori_loop(0, LAYERS // GROUP, one_group, 0)

    for p in range(POLS):
        mixed = mixed_ref[p].reshape(LAYERS * ROWS, 2 * WAVES)
        back = jnp.dot(split_cat(mixed, 1), inv_ref[...], preferred_element_type=F32)
        for c in range(2):
            out_ref[:, 2 * p + c] = back[:, c * CELLS : (c + 1) * CELLS].reshape(LAYERS, ROWS, CELLS)


def mix_kernel(place_ref, rows_ref, green_ref, fwd_ref, inv_ref, out_ref, spec_ref, kern_ref, mixed_ref):
    mix_rows(rows_ref, green_ref, place_ref, fwd_ref, inv_ref, out_ref, spec_ref, kern_ref, mixed_ref)


def sin_pi(v):
    square = v * v
    total = jnp.full_like(v, math.pi**13 / math.factorial(13))
    for order in (11, 9, 7, 5, 3, 1):
        sign = -1.0 if (order // 2) % 2 else 1.0
        total = total * square + sign * math.pi**order / math.factorial(order)
    return total * v


def adjoint_mix_kernel(
    place_ref, first_ref, sent_ref, green_ref, fwd_ref, inv_ref,
    out_ref, rows_ref, spec_ref, kern_ref, mixed_ref,
):
    sent = [sent_ref[:, :, k * CELLS : (k + 1) * CELLS] for k in range(5)]
    cell = sent[4].astype(jnp.int32)
    x_cell = cell >> 7
    wave = first_ref[0] + lax.broadcasted_iota(jnp.int32, (LAYERS, ROWS, CELLS), 1)
    turn = (wave * x_cell) & (WAVES - 1)
    u = (turn.astype(F32) - WAVES / 2) * (2.0 / WAVES)
    size = jnp.abs(u)
    cos = -sin_pi(0.5 - size)
    sin = sin_pi(jnp.minimum(size, 1.0 - size))
    sin = jnp.where(u < 0, sin, -sin)
    for p in range(POLS):
        re, im = sent[2 * p], sent[2 * p + 1]
        rows_ref[:, 2 * p] = re * cos + im * sin
        rows_ref[:, 2 * p + 1] = im * cos - re * sin
    y_ids = lax.broadcasted_iota(jnp.int32, (CELLS, CELLS), 0)
    for j in range(LAYERS):
        y_cell = cell[j] & (CELLS - 1)
        spot = jnp.where(y_ids == y_cell, 1.0, 0.0).astype(BF16)
        values = rows_ref[j].reshape(4 * ROWS, CELLS)
        high = values.astype(BF16)
        low = (values - high.astype(F32)).astype(BF16)
        at_y = lax.dot_general(
            jnp.concatenate([high, low], axis=0), spot, (((1,), (1,)), ((), ())),
            preferred_element_type=F32,
        )
        rows_ref[j] = (at_y[: 4 * ROWS] + at_y[4 * ROWS :]).reshape(4, ROWS, CELLS)
    mix_rows(rows_ref, green_ref, place_ref, fwd_ref, inv_ref, out_ref, spec_ref, kern_ref, mixed_ref)


def x_inverse(rows_ref, table_ref):
    parts = [
        jnp.concatenate(
            [rows_ref[:, 2 * p + c].reshape(WAVES, CELLS) for p in range(POLS)], axis=1
        )
        for c in range(2)
    ]
    waves = jnp.concatenate(parts, axis=0)
    cells = jnp.dot(table_ref[...], split_cat(waves, 0), preferred_element_type=F32)
    return [
        [cells[c * CELLS : (c + 1) * CELLS, p * CELLS : (p + 1) * CELLS] for c in range(2)]
        for p in range(POLS)
    ]


def residual_kernel(rows_ref, field_ref, station_ref, seen_ref, error_ref, table_ref, total_ref, sent_ref):
    scattered = x_inverse(rows_ref, table_ref)
    cell = station_ref[...]
    ids = lax.broadcasted_iota(jnp.int32, (CELLS, CELLS), 0)
    x_spot = jnp.where(ids == (cell >> 7), 1.0, 0.0).astype(BF16)
    y_spot = ids == (cell & (CELLS - 1))
    sent = []
    for p in range(POLS):
        weight = error_ref[0, p] * error_ref[0, p]
        for c in range(2):
            total = field_ref[0, p, c, 0] + scattered[p][c]
            total_ref[2 * p + c] = total
            turned = total.T
            picked = jnp.zeros((CELLS, CELLS), F32)
            for _ in range(3):
                piece = turned.astype(BF16)
                picked = picked + jnp.dot(piece, x_spot, preferred_element_type=F32)
                turned = turned - piece.astype(F32)
            predicted = jnp.sum(jnp.where(y_spot, picked, 0.0), axis=0, keepdims=True)
            resid = (predicted - seen_ref[0, p, c]) / weight
            sent.append(-resid if c else resid)
    sent.append(cell.astype(F32))
    message = jnp.concatenate(sent, axis=1)
    sent_ref[...] = jnp.broadcast_to(message[None], (LAYERS, 1, 5 * CELLS))


def gradient_kernel(rows_ref, total_ref, table_ref, out_ref):
    adjoint = x_inverse(rows_ref, table_ref)
    term = jnp.zeros((CELLS, CELLS), F32)
    for p in range(POLS):
        term = term + (total_ref[2 * p] * adjoint[p][0] - total_ref[2 * p + 1] * adjoint[p][1])
    out_ref[...] = jnp.broadcast_to(term[None], (RING, CELLS, CELLS))


def call(kernel, out_shape, scratch=(), smem=0, operands=()):
    specs = [pl.BlockSpec(memory_space=pltpu.SMEM)] * smem
    specs += [pl.BlockSpec(memory_space=pltpu.VMEM)] * (len(operands) - smem)
    if isinstance(out_shape, list):
        out_specs = [pl.BlockSpec(memory_space=pltpu.VMEM)] * len(out_shape)
    else:
        out_specs = pl.BlockSpec(memory_space=pltpu.VMEM)
    return pl.pallas_call(
        kernel,
        out_shape=out_shape,
        in_specs=specs,
        out_specs=out_specs,
        scratch_shapes=list(scratch),
        compiler_params=pltpu.CompilerParams(vmem_limit_bytes=VMEM_BYTES),
    )(*operands)


def over_layers(values):
    return lax.all_to_all(values, "layer", split_axis=0, concat_axis=0, tiled=True)


def sum_over_freq(copies, size):
    rings = [list(range(r, r + RING)) for r in range(0, size, RING)]
    lines = [list(range(r, size, RING)) for r in range(RING)]
    for groups in (rings, lines):
        parts = lax.all_to_all(
            copies, "freq", split_axis=0, concat_axis=0, tiled=True, axis_index_groups=groups
        )
        total = (parts[0] + parts[1]) + (parts[2] + parts[3])
        copies = jnp.broadcast_to(total[None], copies.shape)
    return total


def per_device(conductivity, background, green, pair_table, stations, observed, data_error, freqs):
    x_fwd, y_fwd, y_inv, x_inv = dft_blocks()
    x_inv = left_table(x_inv)
    y_fwd, y_inv = right_table(y_fwd), right_table(y_inv)
    places = (pair_table * (3 * ROWS)).reshape(-1)
    rows_shape = jax.ShapeDtypeStruct((LAYERS, 4, ROWS, CELLS), F32)
    scratch = (
        pltpu.VMEM((2, LAYERS, 3 * POLS * ROWS, CELLS), F32),
        pltpu.VMEM((2, KERNELS, 3 * ROWS, CELLS), F32),
        pltpu.VMEM((POLS, LAYERS, ROWS, 2 * WAVES), F32),
    )
    rows = pl.pallas_call(
        x_forward_kernel,
        out_shape=rows_shape,
        in_specs=[pl.BlockSpec(memory_space=pl.ANY)] * 3,
        out_specs=pl.BlockSpec(memory_space=pltpu.VMEM),
        scratch_shapes=[
            pltpu.VMEM(conductivity.shape, F32),
            pltpu.VMEM(background.shape, F32),
            pltpu.VMEM(x_fwd.shape, BF16),
            pltpu.SemaphoreType.DMA((3,)),
        ],
        compiler_params=pltpu.CompilerParams(vmem_limit_bytes=FIRST_BYTES),
    )(conductivity, background, x_fwd)
    back = call(
        mix_kernel, rows_shape, scratch, 1,
        (places, over_layers(rows), green, y_fwd, y_inv),
    )
    total, sent = call(
        residual_kernel,
        [
            jax.ShapeDtypeStruct((4, CELLS, CELLS), F32),
            jax.ShapeDtypeStruct((LAYERS, 1, 5 * CELLS), F32),
        ],
        operands=(over_layers(back), background, stations, observed, data_error, x_inv),
    )
    first = (lax.axis_index("layer") * ROWS).astype(jnp.int32).reshape(1)
    back = call(
        adjoint_mix_kernel, rows_shape,
        (pltpu.VMEM((LAYERS, 4, ROWS, CELLS), F32),) + scratch, 2,
        (places, first, over_layers(sent), green, y_fwd, y_inv),
    )
    copies = call(
        gradient_kernel,
        jax.ShapeDtypeStruct((RING, CELLS, CELLS), F32),
        operands=(over_layers(back), total, x_inv),
    )
    return sum_over_freq(copies, freqs)[None]


def solution(mesh):
    in_specs = (
        P("layer", None, None),
        P("freq", None, None, "layer", None, None),
        P("freq", None, None, "layer", None),
        P(),
        P("layer", None),
        P("freq", None, None, "layer", None),
        P("freq", None, "layer", None),
    )
    return jax.shard_map(
        functools.partial(per_device, freqs=mesh.shape["freq"]),
        mesh=mesh, in_specs=in_specs, out_specs=P("layer", None, None), check_vma=False,
    )
```

```python
import functools
import math

import jax
import jax.numpy as jnp
import ml_dtypes
import numpy as np
from jax import lax
from jax.experimental import pallas as pl
from jax.experimental.pallas import tpu as pltpu
from jax.sharding import PartitionSpec as P

CELLS = 128
WAVES = 256
LAYERS = 32
ROWS = 8
KERNELS = 32
POLS = 2
GROUP = 4
STEP = 16
RING = 4
F32 = jnp.float32
BF16 = jnp.bfloat16
VMEM_BYTES = 40 * 1024 * 1024
FIRST_BYTES = 60 * 1024 * 1024


def halves(table):
    high = table.astype(ml_dtypes.bfloat16)
    low = (table - high.astype(np.float64)).astype(ml_dtypes.bfloat16)
    return high, low


def dft_blocks():
    waves = np.arange(WAVES)[:, None]
    cells = np.arange(CELLS)[None, :]
    angles = (waves * cells % WAVES) * (2.0 * math.pi / WAVES)
    cos, sin = np.cos(angles), np.sin(angles)
    x_fwd = np.concatenate(halves(np.concatenate([cos, sin], axis=1)), axis=1)
    y_fwd = np.block([[cos.T, -sin.T], [sin.T, cos.T]])
    y_inv = np.block([[cos, sin], [-sin, cos]]) / WAVES
    x_inv = np.block([[cos.T, -sin.T], [sin.T, cos.T]]) / WAVES
    return x_fwd, y_fwd, y_inv, x_inv


def left_table(table):
    high, low = halves(table)
    return np.concatenate([high, high, low], axis=1)


def right_table(table):
    high, low = halves(table)
    return np.concatenate([high, high, low], axis=0)


def split_cat(values, axis):
    high = values.astype(BF16)
    low = (values - high.astype(F32)).astype(BF16)
    return jnp.concatenate([high, low, high], axis=axis)


def x_forward_kernel(
    cond_hbm, field_hbm, table_hbm, place_any, first_any, out_ref, cond_ref, field_ref, table_ref, sems
):
    del place_any, first_any
    copies = [
        pltpu.make_async_copy(source, target, sems.at[n])
        for n, (source, target) in enumerate(
            ((field_hbm, field_ref), (cond_hbm, cond_ref), (table_hbm, table_ref))
        )
    ]
    for copy in copies:
        copy.start()
    copies[0].wait()
    copies[1].wait()
    cond = cond_ref[0]
    high, low = [], []
    for c in range(2):
        part = jnp.concatenate([cond * field_ref[0, p, c, 0] for p in range(POLS)], axis=1)
        high.append(part.astype(BF16))
        low.append((part - high[c].astype(F32)).astype(BF16))
    stacks = [
        jnp.concatenate([jnp.concatenate([part[0], part[1]], axis=1), jnp.concatenate([part[1], -part[0]], axis=1)], axis=0)
        for part in (high, low)
    ]
    cells = jnp.concatenate([stacks[0], stacks[1], stacks[0]], axis=0)
    copies[2].wait()
    table = table_ref[...]
    table = jnp.concatenate([table[:, :WAVES], table], axis=1)
    rows = jnp.dot(table, cells, preferred_element_type=F32)
    for c in range(2):
        for p in range(POLS):
            at = (c * POLS + p) * CELLS
            out_ref[:, 2 * p + c] = rows[:, at : at + CELLS].reshape(LAYERS, ROWS, CELLS)


def mix_rows(rows_ref, green_ref, place_ref, fwd_ref, inv_ref, out_ref, spec_ref, kern_ref, mixed_ref):
    lanes = [slice(h * CELLS, (h + 1) * CELLS) for h in range(2)]
    for h in range(2):
        g_re = green_ref[0, 0, :, :, lanes[h]]
        g_im = green_ref[0, 1, :, :, lanes[h]]
        kern_ref[h, :, 0:ROWS] = g_re + g_im
        kern_ref[h, :, ROWS : 2 * ROWS] = g_re
        kern_ref[h, :, 2 * ROWS :] = g_im
    for p in range(POLS):
        flat = [rows_ref[:, 2 * p + c].reshape(LAYERS * ROWS, CELLS) for c in range(2)]
        both = jnp.concatenate(flat, axis=1)
        spec = jnp.dot(split_cat(both, 1), fwd_ref[...], preferred_element_type=F32)
        for h in range(2):
            re = spec[:, h * CELLS : (h + 1) * CELLS].reshape(LAYERS, ROWS, CELLS)
            im = spec[:, WAVES + h * CELLS : WAVES + (h + 1) * CELLS].reshape(LAYERS, ROWS, CELLS)
            for k, value in enumerate((re, im - re, re + im)):
                at = (3 * p + k) * ROWS
                spec_ref[h, :, at : at + ROWS] = value

    kern = [kern_ref.at[h].reshape(KERNELS * 3 * ROWS, CELLS) for h in range(2)]
    for h in range(2):

        def one_group(group, carry, h=h):
            first = group * GROUP

            def some_sources(chunk, sums):
                sums = list(sums)
                base = first * LAYERS + chunk * STEP
                for s in range(STEP):
                    j = chunk * STEP + s
                    src = [spec_ref[h, j, k * ROWS : (k + 1) * ROWS] for k in range(3 * POLS)]
                    for r in range(GROUP):
                        place = place_ref[base + (r * LAYERS + s)]
                        for k in range(3):
                            row = pl.multiple_of(place + k * ROWS, ROWS)
                            factor = kern[h][pl.ds(row, ROWS), :]
                            for p in range(POLS):
                                at = (r * POLS + p) * 3 + k
                                sums[at] = sums[at] + factor * src[3 * p + k]
                return tuple(sums)

            zero = jnp.zeros((ROWS, CELLS), F32)
            sums = lax.fori_loop(
                0, LAYERS // STEP, some_sources, (zero,) * (GROUP * POLS * 3)
            )
            for r in range(GROUP):
                for p in range(POLS):
                    one, two, three = sums[(r * POLS + p) * 3 : (r * POLS + p) * 3 + 3]
                    mixed_ref[p, first + r, :, h * CELLS : (h + 1) * CELLS] = one - three
                    mixed_ref[p, first + r, :, WAVES + h * CELLS : WAVES + (h + 1) * CELLS] = one + two
            return carry

        lax.fori_loop(0, LAYERS // GROUP, one_group, 0)

    for p in range(POLS):
        mixed = mixed_ref[p].reshape(LAYERS * ROWS, 2 * WAVES)
        back = jnp.dot(split_cat(mixed, 1), inv_ref[...], preferred_element_type=F32)
        for c in range(2):
            out_ref[:, 2 * p + c] = back[:, c * CELLS : (c + 1) * CELLS].reshape(LAYERS, ROWS, CELLS)


def mix_kernel(place_ref, rows_ref, green_ref, fwd_ref, inv_ref, out_ref, spec_ref, kern_ref, mixed_ref):
    mix_rows(rows_ref, green_ref, place_ref, fwd_ref, inv_ref, out_ref, spec_ref, kern_ref, mixed_ref)


def sin_pi(v):
    square = v * v
    total = jnp.full_like(v, math.pi**13 / math.factorial(13))
    for order in (11, 9, 7, 5, 3, 1):
        sign = -1.0 if (order // 2) % 2 else 1.0
        total = total * square + sign * math.pi**order / math.factorial(order)
    return total * v


def adjoint_mix_kernel(
    place_ref, first_ref, sent_ref, green_ref, fwd_ref, inv_ref,
    out_ref, rows_ref, spec_ref, kern_ref, mixed_ref,
):
    sent = [sent_ref[:, :, k * CELLS : (k + 1) * CELLS] for k in range(5)]
    cell = sent[4].astype(jnp.int32)
    x_cell = cell >> 7
    wave = first_ref[0] + lax.broadcasted_iota(jnp.int32, (LAYERS, ROWS, CELLS), 1)
    turn = (wave * x_cell) & (WAVES - 1)
    u = (turn.astype(F32) - WAVES / 2) * (2.0 / WAVES)
    size = jnp.abs(u)
    cos = -sin_pi(0.5 - size)
    sin = sin_pi(jnp.minimum(size, 1.0 - size))
    sin = jnp.where(u < 0, sin, -sin)
    for p in range(POLS):
        re, im = sent[2 * p], sent[2 * p + 1]
        rows_ref[:, 2 * p] = re * cos + im * sin
        rows_ref[:, 2 * p + 1] = im * cos - re * sin
    y_ids = lax.broadcasted_iota(jnp.int32, (CELLS, CELLS), 0)
    for j in range(LAYERS):
        y_cell = cell[j] & (CELLS - 1)
        spot = jnp.where(y_ids == y_cell, 1.0, 0.0).astype(BF16)
        values = rows_ref[j].reshape(4 * ROWS, CELLS)
        high = values.astype(BF16)
        low = (values - high.astype(F32)).astype(BF16)
        at_y = lax.dot_general(
            jnp.concatenate([high, low], axis=0), spot, (((1,), (1,)), ((), ())),
            preferred_element_type=F32,
        )
        rows_ref[j] = (at_y[: 4 * ROWS] + at_y[4 * ROWS :]).reshape(4, ROWS, CELLS)
    mix_rows(rows_ref, green_ref, place_ref, fwd_ref, inv_ref, out_ref, spec_ref, kern_ref, mixed_ref)


def x_inverse(rows_ref, table_ref):
    parts = [
        jnp.concatenate(
            [rows_ref[:, 2 * p + c].reshape(WAVES, CELLS) for p in range(POLS)], axis=1
        )
        for c in range(2)
    ]
    waves = jnp.concatenate(parts, axis=0)
    cells = jnp.dot(table_ref[...], split_cat(waves, 0), preferred_element_type=F32)
    return [
        [cells[c * CELLS : (c + 1) * CELLS, p * CELLS : (p + 1) * CELLS] for c in range(2)]
        for p in range(POLS)
    ]


def residual_kernel(rows_ref, field_ref, station_ref, seen_ref, error_ref, table_ref, total_ref, sent_ref):
    scattered = x_inverse(rows_ref, table_ref)
    cell = station_ref[...]
    ids = lax.broadcasted_iota(jnp.int32, (CELLS, CELLS), 0)
    x_spot = jnp.where(ids == (cell >> 7), 1.0, 0.0).astype(BF16)
    y_spot = ids == (cell & (CELLS - 1))
    sent = []
    for p in range(POLS):
        weight = error_ref[0, p] * error_ref[0, p]
        for c in range(2):
            total = field_ref[0, p, c, 0] + scattered[p][c]
            total_ref[2 * p + c] = total
            turned = total.T
            picked = jnp.zeros((CELLS, CELLS), F32)
            for _ in range(3):
                piece = turned.astype(BF16)
                picked = picked + jnp.dot(piece, x_spot, preferred_element_type=F32)
                turned = turned - piece.astype(F32)
            predicted = jnp.sum(jnp.where(y_spot, picked, 0.0), axis=0, keepdims=True)
            resid = (predicted - seen_ref[0, p, c]) / weight
            sent.append(-resid if c else resid)
    sent.append(cell.astype(F32))
    message = jnp.concatenate(sent, axis=1)
    sent_ref[...] = jnp.broadcast_to(message[None], (LAYERS, 1, 5 * CELLS))


def gradient_kernel(rows_ref, total_ref, table_ref, out_ref):
    adjoint = x_inverse(rows_ref, table_ref)
    term = jnp.zeros((CELLS, CELLS), F32)
    for p in range(POLS):
        term = term + (total_ref[2 * p] * adjoint[p][0] - total_ref[2 * p + 1] * adjoint[p][1])
    out_ref[...] = jnp.broadcast_to(term[None], (RING, CELLS, CELLS))


def call(kernel, out_shape, scratch=(), smem=0, operands=()):
    specs = [pl.BlockSpec(memory_space=pltpu.SMEM)] * smem
    specs += [pl.BlockSpec(memory_space=pltpu.VMEM)] * (len(operands) - smem)
    if isinstance(out_shape, list):
        out_specs = [pl.BlockSpec(memory_space=pltpu.VMEM)] * len(out_shape)
    else:
        out_specs = pl.BlockSpec(memory_space=pltpu.VMEM)
    return pl.pallas_call(
        kernel,
        out_shape=out_shape,
        in_specs=specs,
        out_specs=out_specs,
        scratch_shapes=list(scratch),
        compiler_params=pltpu.CompilerParams(vmem_limit_bytes=VMEM_BYTES),
    )(*operands)


def over_layers(values):
    return lax.all_to_all(values, "layer", split_axis=0, concat_axis=0, tiled=True)


def sum_over_freq(copies, size):
    rings = [list(range(r, r + RING)) for r in range(0, size, RING)]
    lines = [list(range(r, size, RING)) for r in range(RING)]
    for groups in (rings, lines):
        parts = lax.all_to_all(
            copies, "freq", split_axis=0, concat_axis=0, tiled=True, axis_index_groups=groups
        )
        total = (parts[0] + parts[1]) + (parts[2] + parts[3])
        copies = jnp.broadcast_to(total[None], copies.shape)
    return total


def per_device(conductivity, background, green, pair_table, stations, observed, data_error, freqs):
    x_fwd, y_fwd, y_inv, x_inv = dft_blocks()
    x_inv = left_table(x_inv)
    y_fwd, y_inv = right_table(y_fwd), right_table(y_inv)
    places = (pair_table * (3 * ROWS)).reshape(-1)
    first = (lax.axis_index("layer") * ROWS).astype(jnp.int32).reshape(1)
    rows_shape = jax.ShapeDtypeStruct((LAYERS, 4, ROWS, CELLS), F32)
    scratch = (
        pltpu.VMEM((2, LAYERS, 3 * POLS * ROWS, CELLS), F32),
        pltpu.VMEM((2, KERNELS, 3 * ROWS, CELLS), F32),
        pltpu.VMEM((POLS, LAYERS, ROWS, 2 * WAVES), F32),
    )
    rows = pl.pallas_call(
        x_forward_kernel,
        out_shape=rows_shape,
        in_specs=[pl.BlockSpec(memory_space=pltpu.HBM)] * 3
        + [pl.BlockSpec(memory_space=pl.ANY)] * 2,
        out_specs=pl.BlockSpec(memory_space=pltpu.VMEM),
        scratch_shapes=[
            pltpu.VMEM(conductivity.shape, F32),
            pltpu.VMEM(background.shape, F32),
            pltpu.VMEM(x_fwd.shape, BF16),
            pltpu.SemaphoreType.DMA((3,)),
        ],
        compiler_params=pltpu.CompilerParams(vmem_limit_bytes=FIRST_BYTES),
    )(conductivity, background, x_fwd, places, first)
    back = call(
        mix_kernel, rows_shape, scratch, 1,
        (places, over_layers(rows), green, y_fwd, y_inv),
    )
    total, sent = call(
        residual_kernel,
        [
            jax.ShapeDtypeStruct((4, CELLS, CELLS), F32),
            jax.ShapeDtypeStruct((LAYERS, 1, 5 * CELLS), F32),
        ],
        operands=(over_layers(back), background, stations, observed, data_error, x_inv),
    )
    back = call(
        adjoint_mix_kernel, rows_shape,
        (pltpu.VMEM((LAYERS, 4, ROWS, CELLS), F32),) + scratch, 2,
        (places, first, over_layers(sent), green, y_fwd, y_inv),
    )
    copies = call(
        gradient_kernel,
        jax.ShapeDtypeStruct((RING, CELLS, CELLS), F32),
        operands=(over_layers(back), total, x_inv),
    )
    return sum_over_freq(copies, freqs)[None]


def solution(mesh):
    in_specs = (
        P("layer", None, None),
        P("freq", None, None, "layer", None, None),
        P("freq", None, None, "layer", None),
        P(),
        P("layer", None),
        P("freq", None, None, "layer", None),
        P("freq", None, "layer", None),
    )
    return jax.shard_map(
        functools.partial(per_device, freqs=mesh.shape["freq"]),
        mesh=mesh, in_specs=in_specs, out_specs=P("layer", None, None), check_vma=False,
    )
```

```python
import functools
import math

import jax
import jax.numpy as jnp
import ml_dtypes
import numpy as np
from jax import lax
from jax.experimental import pallas as pl
from jax.experimental.pallas import tpu as pltpu
from jax.sharding import PartitionSpec as P

CELLS = 128
WAVES = 256
LAYERS = 32
ROWS = 8
KERNELS = 32
POLS = 2
GROUP = 4
STEP = 16
RING = 4
F32 = jnp.float32
BF16 = jnp.bfloat16
VMEM_BYTES = 40 * 1024 * 1024
FIRST_BYTES = 60 * 1024 * 1024


def halves(table):
    high = table.astype(ml_dtypes.bfloat16)
    low = (table - high.astype(np.float64)).astype(ml_dtypes.bfloat16)
    return high, low


def dft_blocks():
    waves = np.arange(WAVES)[:, None]
    cells = np.arange(CELLS)[None, :]
    angles = (waves * cells % WAVES) * (2.0 * math.pi / WAVES)
    cos, sin = np.cos(angles), np.sin(angles)
    x_fwd = np.concatenate([cos, sin], axis=1)
    y_fwd = np.block([[cos.T, -sin.T], [sin.T, cos.T]])
    y_inv = np.block([[cos, sin], [-sin, cos]]) / WAVES
    x_inv = np.block([[cos.T, -sin.T], [sin.T, cos.T]]) / WAVES
    y_both = np.concatenate(
        [np.concatenate(halves(y_fwd), axis=0), np.concatenate(halves(y_inv), axis=1)], axis=0
    )
    return np.concatenate(halves(x_fwd), axis=1), y_both, np.concatenate(halves(x_inv), axis=1)


def thrice(table, axis):
    high, low = jnp.split(table, 2, axis=axis)
    return jnp.concatenate([high, high, low], axis=axis)


def split_cat(values, axis):
    high = values.astype(BF16)
    low = (values - high.astype(F32)).astype(BF16)
    return jnp.concatenate([high, low, high], axis=axis)


def x_forward_kernel(
    cond_hbm, field_hbm, table_hbm, pair_hbm, first_any,
    out_ref, place_ref, cond_ref, field_ref, table_ref, pair_ref, sems,
):
    del first_any
    moves = ((field_hbm, field_ref), (cond_hbm, cond_ref), (table_hbm, table_ref), (pair_hbm, pair_ref))
    copies = [
        pltpu.make_async_copy(source, target, sems.at[n])
        for n, (source, target) in enumerate(moves)
    ]
    for copy in copies:
        copy.start()
    copies[0].wait()
    copies[1].wait()
    cond = cond_ref[0]
    high, low = [], []
    for c in range(2):
        part = jnp.concatenate([cond * field_ref[0, p, c, 0] for p in range(POLS)], axis=1)
        high.append(part.astype(BF16))
        low.append((part - high[c].astype(F32)).astype(BF16))
    stacks = [
        jnp.concatenate([jnp.concatenate([part[0], part[1]], axis=1), jnp.concatenate([part[1], -part[0]], axis=1)], axis=0)
        for part in (high, low)
    ]
    cells = jnp.concatenate([stacks[0], stacks[1], stacks[0]], axis=0)
    copies[3].wait()
    place_ref[...] = pair_ref[...] * (3 * ROWS)
    copies[2].wait()
    rows = jnp.dot(thrice(table_ref[...], 1), cells, preferred_element_type=F32)
    for c in range(2):
        for p in range(POLS):
            at = (c * POLS + p) * CELLS
            out_ref[:, 2 * p + c] = rows[:, at : at + CELLS].reshape(LAYERS, ROWS, CELLS)


def mix_rows(rows_ref, green_ref, place_ref, table_ref, out_ref, spec_ref, kern_ref, mixed_ref):
    lanes = [slice(h * CELLS, (h + 1) * CELLS) for h in range(2)]
    for h in range(2):
        g_re = green_ref[0, 0, :, :, lanes[h]]
        g_im = green_ref[0, 1, :, :, lanes[h]]
        kern_ref[h, :, 0:ROWS] = g_re + g_im
        kern_ref[h, :, ROWS : 2 * ROWS] = g_re
        kern_ref[h, :, 2 * ROWS :] = g_im
    forward = thrice(table_ref[: 2 * WAVES], 0)
    for p in range(POLS):
        flat = [rows_ref[:, 2 * p + c].reshape(LAYERS * ROWS, CELLS) for c in range(2)]
        both = jnp.concatenate(flat, axis=1)
        spec = jnp.dot(split_cat(both, 1), forward, preferred_element_type=F32)
        for h in range(2):
            re = spec[:, h * CELLS : (h + 1) * CELLS].reshape(LAYERS, ROWS, CELLS)
            im = spec[:, WAVES + h * CELLS : WAVES + (h + 1) * CELLS].reshape(LAYERS, ROWS, CELLS)
            for k, value in enumerate((re, im - re, re + im)):
                at = (3 * p + k) * ROWS
                spec_ref[h, :, at : at + ROWS] = value

    kern = [kern_ref.at[h].reshape(KERNELS * 3 * ROWS, CELLS) for h in range(2)]
    for h in range(2):

        def one_group(group, carry, h=h):
            first = group * GROUP

            def some_sources(chunk, sums):
                sums = list(sums)
                for s in range(STEP):
                    j = chunk * STEP + s
                    src = [spec_ref[h, j, k * ROWS : (k + 1) * ROWS] for k in range(3 * POLS)]
                    for r in range(GROUP):
                        place = place_ref[first + r, j]
                        for k in range(3):
                            row = pl.multiple_of(place + k * ROWS, ROWS)
                            factor = kern[h][pl.ds(row, ROWS), :]
                            for p in range(POLS):
                                at = (r * POLS + p) * 3 + k
                                sums[at] = sums[at] + factor * src[3 * p + k]
                return tuple(sums)

            zero = jnp.zeros((ROWS, CELLS), F32)
            sums = lax.fori_loop(
                0, LAYERS // STEP, some_sources, (zero,) * (GROUP * POLS * 3)
            )
            for r in range(GROUP):
                for p in range(POLS):
                    one, two, three = sums[(r * POLS + p) * 3 : (r * POLS + p) * 3 + 3]
                    mixed_ref[p, first + r, :, h * CELLS : (h + 1) * CELLS] = one - three
                    mixed_ref[p, first + r, :, WAVES + h * CELLS : WAVES + (h + 1) * CELLS] = one + two
            return carry

        lax.fori_loop(0, LAYERS // GROUP, one_group, 0)

    high, low = table_ref[2 * WAVES :, :WAVES], table_ref[2 * WAVES :, WAVES:]
    inverse = jnp.concatenate([high, high, low], axis=0)
    for p in range(POLS):
        mixed = mixed_ref[p].reshape(LAYERS * ROWS, 2 * WAVES)
        back = jnp.dot(split_cat(mixed, 1), inverse, preferred_element_type=F32)
        for c in range(2):
            out_ref[:, 2 * p + c] = back[:, c * CELLS : (c + 1) * CELLS].reshape(LAYERS, ROWS, CELLS)


def mix_kernel(place_ref, rows_ref, green_ref, table_ref, out_ref, spec_ref, kern_ref, mixed_ref):
    mix_rows(rows_ref, green_ref, place_ref, table_ref, out_ref, spec_ref, kern_ref, mixed_ref)


def sin_pi(v):
    square = v * v
    total = jnp.full_like(v, math.pi**13 / math.factorial(13))
    for order in (11, 9, 7, 5, 3, 1):
        sign = -1.0 if (order // 2) % 2 else 1.0
        total = total * square + sign * math.pi**order / math.factorial(order)
    return total * v


def adjoint_mix_kernel(
    place_ref, first_ref, sent_ref, green_ref, table_ref,
    out_ref, rows_ref, spec_ref, kern_ref, mixed_ref,
):
    sent = [sent_ref[:, :, k * CELLS : (k + 1) * CELLS] for k in range(5)]
    cell = sent[4].astype(jnp.int32)
    x_cell = cell >> 7
    wave = first_ref[0] + lax.broadcasted_iota(jnp.int32, (LAYERS, ROWS, CELLS), 1)
    turn = (wave * x_cell) & (WAVES - 1)
    u = (turn.astype(F32) - WAVES / 2) * (2.0 / WAVES)
    size = jnp.abs(u)
    cos = -sin_pi(0.5 - size)
    sin = sin_pi(jnp.minimum(size, 1.0 - size))
    sin = jnp.where(u < 0, sin, -sin)
    for p in range(POLS):
        re, im = sent[2 * p], sent[2 * p + 1]
        rows_ref[:, 2 * p] = re * cos + im * sin
        rows_ref[:, 2 * p + 1] = im * cos - re * sin
    y_ids = lax.broadcasted_iota(jnp.int32, (CELLS, CELLS), 0)
    for j in range(LAYERS):
        y_cell = cell[j] & (CELLS - 1)
        spot = jnp.where(y_ids == y_cell, 1.0, 0.0).astype(BF16)
        values = rows_ref[j].reshape(4 * ROWS, CELLS)
        high = values.astype(BF16)
        low = (values - high.astype(F32)).astype(BF16)
        at_y = lax.dot_general(
            jnp.concatenate([high, low], axis=0), spot, (((1,), (1,)), ((), ())),
            preferred_element_type=F32,
        )
        rows_ref[j] = (at_y[: 4 * ROWS] + at_y[4 * ROWS :]).reshape(4, ROWS, CELLS)
    mix_rows(rows_ref, green_ref, place_ref, table_ref, out_ref, spec_ref, kern_ref, mixed_ref)


def x_inverse(rows_ref, table_ref):
    parts = [
        jnp.concatenate(
            [rows_ref[:, 2 * p + c].reshape(WAVES, CELLS) for p in range(POLS)], axis=1
        )
        for c in range(2)
    ]
    waves = jnp.concatenate(parts, axis=0)
    cells = jnp.dot(thrice(table_ref[...], 1), split_cat(waves, 0), preferred_element_type=F32)
    return [
        [cells[c * CELLS : (c + 1) * CELLS, p * CELLS : (p + 1) * CELLS] for c in range(2)]
        for p in range(POLS)
    ]


def residual_kernel(rows_ref, field_ref, station_ref, seen_ref, error_ref, table_ref, total_ref, sent_ref):
    scattered = x_inverse(rows_ref, table_ref)
    cell = station_ref[...]
    ids = lax.broadcasted_iota(jnp.int32, (CELLS, CELLS), 0)
    x_spot = jnp.where(ids == (cell >> 7), 1.0, 0.0).astype(BF16)
    y_spot = ids == (cell & (CELLS - 1))
    sent = []
    for p in range(POLS):
        weight = error_ref[0, p] * error_ref[0, p]
        for c in range(2):
            total = field_ref[0, p, c, 0] + scattered[p][c]
            total_ref[2 * p + c] = total
            turned = total.T
            picked = jnp.zeros((CELLS, CELLS), F32)
            for _ in range(3):
                piece = turned.astype(BF16)
                picked = picked + jnp.dot(piece, x_spot, preferred_element_type=F32)
                turned = turned - piece.astype(F32)
            predicted = jnp.sum(jnp.where(y_spot, picked, 0.0), axis=0, keepdims=True)
            resid = (predicted - seen_ref[0, p, c]) / weight
            sent.append(-resid if c else resid)
    sent.append(cell.astype(F32))
    message = jnp.concatenate(sent, axis=1)
    sent_ref[...] = jnp.broadcast_to(message[None], (LAYERS, 1, 5 * CELLS))


def gradient_kernel(rows_ref, total_ref, table_ref, out_ref):
    adjoint = x_inverse(rows_ref, table_ref)
    term = jnp.zeros((CELLS, CELLS), F32)
    for p in range(POLS):
        term = term + (total_ref[2 * p] * adjoint[p][0] - total_ref[2 * p + 1] * adjoint[p][1])
    out_ref[...] = jnp.broadcast_to(term[None], (RING, CELLS, CELLS))


def call(kernel, out_shape, scratch=(), smem=0, operands=()):
    specs = [pl.BlockSpec(memory_space=pltpu.SMEM)] * smem
    specs += [pl.BlockSpec(memory_space=pltpu.VMEM)] * (len(operands) - smem)
    if isinstance(out_shape, list):
        out_specs = [pl.BlockSpec(memory_space=pltpu.VMEM)] * len(out_shape)
    else:
        out_specs = pl.BlockSpec(memory_space=pltpu.VMEM)
    return pl.pallas_call(
        kernel,
        out_shape=out_shape,
        in_specs=specs,
        out_specs=out_specs,
        scratch_shapes=list(scratch),
        compiler_params=pltpu.CompilerParams(vmem_limit_bytes=VMEM_BYTES),
    )(*operands)


def over_layers(values):
    return lax.all_to_all(values, "layer", split_axis=0, concat_axis=0, tiled=True)


def sum_over_freq(copies, size):
    rings = [list(range(r, r + RING)) for r in range(0, size, RING)]
    lines = [[r + RING * k for k in (1, 0, 2, 3)] for r in range(RING)]
    for groups in (rings, lines):
        parts = lax.all_to_all(
            copies, "freq", split_axis=0, concat_axis=0, tiled=True, axis_index_groups=groups
        )
        total = (parts[0] + parts[1]) + (parts[2] + parts[3])
        copies = jnp.broadcast_to(total[None], copies.shape)
    return total


def per_device(conductivity, background, green, pair_table, stations, observed, data_error, freqs):
    x_fwd, y_both, x_inv = dft_blocks()
    first = (lax.axis_index("layer") * ROWS).astype(jnp.int32).reshape(1)
    rows_shape = jax.ShapeDtypeStruct((LAYERS, 4, ROWS, CELLS), F32)
    scratch = (
        pltpu.VMEM((2, LAYERS, 3 * POLS * ROWS, CELLS), F32),
        pltpu.VMEM((2, KERNELS, 3 * ROWS, CELLS), F32),
        pltpu.VMEM((POLS, LAYERS, ROWS, 2 * WAVES), F32),
    )
    rows, places = pl.pallas_call(
        x_forward_kernel,
        out_shape=[rows_shape, jax.ShapeDtypeStruct(pair_table.shape, jnp.int32)],
        in_specs=[pl.BlockSpec(memory_space=pl.ANY)] * 5,
        out_specs=[pl.BlockSpec(memory_space=pltpu.VMEM)] * 2,
        scratch_shapes=[
            pltpu.VMEM(conductivity.shape, F32),
            pltpu.VMEM(background.shape, F32),
            pltpu.VMEM(x_fwd.shape, BF16),
            pltpu.VMEM(pair_table.shape, jnp.int32),
            pltpu.SemaphoreType.DMA((4,)),
        ],
        compiler_params=pltpu.CompilerParams(vmem_limit_bytes=FIRST_BYTES),
    )(conductivity, background, x_fwd, pair_table, first)
    back = call(
        mix_kernel, rows_shape, scratch, 1,
        (places, over_layers(rows), green, y_both),
    )
    total, sent = call(
        residual_kernel,
        [
            jax.ShapeDtypeStruct((4, CELLS, CELLS), F32),
            jax.ShapeDtypeStruct((LAYERS, 1, 5 * CELLS), F32),
        ],
        operands=(over_layers(back), background, stations, observed, data_error, x_inv),
    )
    back = call(
        adjoint_mix_kernel, rows_shape,
        (pltpu.VMEM((LAYERS, 4, ROWS, CELLS), F32),) + scratch, 2,
        (places, first, over_layers(sent), green, y_both),
    )
    copies = call(
        gradient_kernel,
        jax.ShapeDtypeStruct((RING, CELLS, CELLS), F32),
        operands=(over_layers(back), total, x_inv),
    )
    return sum_over_freq(copies, freqs)[None]


def solution(mesh):
    in_specs = (
        P("layer", None, None),
        P("freq", None, None, "layer", None, None),
        P("freq", None, None, "layer", None),
        P(),
        P("layer", None),
        P("freq", None, None, "layer", None),
        P("freq", None, "layer", None),
    )
    return jax.shard_map(
        functools.partial(per_device, freqs=mesh.shape["freq"]),
        mesh=mesh, in_specs=in_specs, out_specs=P("layer", None, None), check_vma=False,
    )
```

```python
import functools
import math

import jax
import jax.numpy as jnp
import ml_dtypes
import numpy as np
from jax import lax
from jax.experimental import pallas as pl
from jax.experimental.pallas import tpu as pltpu
from jax.sharding import PartitionSpec as P

CELLS = 128
WAVES = 256
LAYERS = 32
ROWS = 8
KERNELS = 32
POLS = 2
GROUP = 4
STEP = 16
RING = 4
SIN_PI = (0.0776576603, -0.5982912856, 2.5500775232, -5.1677100835, 3.1415926401)
F32 = jnp.float32
BF16 = jnp.bfloat16
VMEM_BYTES = 40 * 1024 * 1024
FIRST_BYTES = 60 * 1024 * 1024


def halves(table):
    high = table.astype(ml_dtypes.bfloat16)
    low = (table - high.astype(np.float64)).astype(ml_dtypes.bfloat16)
    return high, low


def dft_blocks():
    waves = np.arange(WAVES)[:, None]
    cells = np.arange(CELLS)[None, :]
    angles = (waves * cells % WAVES) * (2.0 * math.pi / WAVES)
    cos, sin = np.cos(angles), np.sin(angles)
    x_fwd = np.concatenate([cos, sin], axis=1)
    y_fwd = np.block([[cos.T, -sin.T], [sin.T, cos.T]])
    y_inv = np.block([[cos, sin], [-sin, cos]]) / WAVES
    x_inv = np.block([[cos.T, -sin.T], [sin.T, cos.T]]) / WAVES
    y_both = np.concatenate(
        [np.concatenate(halves(y_fwd), axis=0), np.concatenate(halves(y_inv), axis=1)], axis=0
    )
    return np.concatenate(halves(x_fwd), axis=1), y_both, np.concatenate(halves(x_inv), axis=1)


def thrice(table, axis):
    high, low = jnp.split(table, 2, axis=axis)
    return jnp.concatenate([high, high, low], axis=axis)


def split_cat(values, axis):
    high = values.astype(BF16)
    low = (values - high.astype(F32)).astype(BF16)
    return jnp.concatenate([high, low, high], axis=axis)


def x_forward_kernel(
    cond_hbm, field_hbm, table_hbm, pair_hbm, first_any,
    out_ref, place_ref, cond_ref, field_ref, table_ref, pair_ref, sems,
):
    del first_any
    moves = ((field_hbm, field_ref), (cond_hbm, cond_ref), (table_hbm, table_ref), (pair_hbm, pair_ref))
    copies = [
        pltpu.make_async_copy(source, target, sems.at[n])
        for n, (source, target) in enumerate(moves)
    ]
    for copy in copies:
        copy.start()
    copies[0].wait()
    copies[1].wait()
    cond = cond_ref[0]
    high, low = [], []
    for c in range(2):
        part = jnp.concatenate([cond * field_ref[0, p, c, 0] for p in range(POLS)], axis=1)
        high.append(part.astype(BF16))
        low.append((part - high[c].astype(F32)).astype(BF16))
    stacks = [
        jnp.concatenate([jnp.concatenate([part[0], part[1]], axis=1), jnp.concatenate([part[1], -part[0]], axis=1)], axis=0)
        for part in (high, low)
    ]
    cells = jnp.concatenate([stacks[0], stacks[1], stacks[0]], axis=0)
    copies[3].wait()
    place_ref[...] = pair_ref[...] * (3 * ROWS)
    copies[2].wait()
    rows = jnp.dot(thrice(table_ref[...], 1), cells, preferred_element_type=F32)
    for c in range(2):
        for p in range(POLS):
            at = (c * POLS + p) * CELLS
            out_ref[:, 2 * p + c] = rows[:, at : at + CELLS].reshape(LAYERS, ROWS, CELLS)


def mix_rows(rows_ref, green_ref, place_ref, table_ref, out_ref, spec_ref, kern_ref, mixed_ref):
    lanes = [slice(h * CELLS, (h + 1) * CELLS) for h in range(2)]
    forward = thrice(table_ref[: 2 * WAVES], 0)
    for p in range(POLS):
        flat = [rows_ref[:, 2 * p + c].reshape(LAYERS * ROWS, CELLS) for c in range(2)]
        both = jnp.concatenate(flat, axis=1)
        spec = jnp.dot(split_cat(both, 1), forward, preferred_element_type=F32)
        h = p
        g_re = green_ref[0, 0, :, :, lanes[h]]
        g_im = green_ref[0, 1, :, :, lanes[h]]
        kern_ref[h, :, 0:ROWS] = g_re + g_im
        kern_ref[h, :, ROWS : 2 * ROWS] = g_re
        kern_ref[h, :, 2 * ROWS :] = g_im
        for h in range(2):
            re = spec[:, h * CELLS : (h + 1) * CELLS].reshape(LAYERS, ROWS, CELLS)
            im = spec[:, WAVES + h * CELLS : WAVES + (h + 1) * CELLS].reshape(LAYERS, ROWS, CELLS)
            for k, value in enumerate((re, im - re, re + im)):
                at = (3 * p + k) * ROWS
                spec_ref[h, :, at : at + ROWS] = value

    kern = [kern_ref.at[h].reshape(KERNELS * 3 * ROWS, CELLS) for h in range(2)]
    for h in range(2):

        def one_group(group, carry, h=h):
            first = group * GROUP

            def some_sources(chunk, sums):
                sums = list(sums)
                for s in range(STEP):
                    j = chunk * STEP + s
                    src = [spec_ref[h, j, k * ROWS : (k + 1) * ROWS] for k in range(3 * POLS)]
                    for r in range(GROUP):
                        place = place_ref[first + r, j]
                        for k in range(3):
                            row = pl.multiple_of(place + k * ROWS, ROWS)
                            factor = kern[h][pl.ds(row, ROWS), :]
                            for p in range(POLS):
                                at = (r * POLS + p) * 3 + k
                                sums[at] = sums[at] + factor * src[3 * p + k]
                return tuple(sums)

            zero = jnp.zeros((ROWS, CELLS), F32)
            sums = lax.fori_loop(
                0, LAYERS // STEP, some_sources, (zero,) * (GROUP * POLS * 3)
            )
            for r in range(GROUP):
                for p in range(POLS):
                    one, two, three = sums[(r * POLS + p) * 3 : (r * POLS + p) * 3 + 3]
                    mixed_ref[p, first + r, :, h * CELLS : (h + 1) * CELLS] = one - three
                    mixed_ref[p, first + r, :, WAVES + h * CELLS : WAVES + (h + 1) * CELLS] = one + two
            return carry

        lax.fori_loop(0, LAYERS // GROUP, one_group, 0)

    high, low = table_ref[2 * WAVES :, :WAVES], table_ref[2 * WAVES :, WAVES:]
    inverse = jnp.concatenate([high, high, low], axis=0)
    for p in range(POLS):
        mixed = mixed_ref[p].reshape(LAYERS * ROWS, 2 * WAVES)
        back = jnp.dot(split_cat(mixed, 1), inverse, preferred_element_type=F32)
        for c in range(2):
            out_ref[:, 2 * p + c] = back[:, c * CELLS : (c + 1) * CELLS].reshape(LAYERS, ROWS, CELLS)


def mix_kernel(place_ref, rows_ref, green_ref, table_ref, out_ref, spec_ref, kern_ref, mixed_ref):
    mix_rows(rows_ref, green_ref, place_ref, table_ref, out_ref, spec_ref, kern_ref, mixed_ref)


def sin_pi(v):
    square = v * v
    total = jnp.full_like(v, SIN_PI[0])
    for factor in SIN_PI[1:]:
        total = total * square + factor
    return total * v


def adjoint_mix_kernel(
    place_ref, first_ref, sent_ref, green_ref, table_ref,
    out_ref, rows_ref, spec_ref, kern_ref, mixed_ref,
):
    sent = [sent_ref[:, :, k * CELLS : (k + 1) * CELLS] for k in range(5)]
    cell = sent[4].astype(jnp.int32)
    x_cell = cell >> 7
    wave = first_ref[0] + lax.broadcasted_iota(jnp.int32, (LAYERS, ROWS, CELLS), 1)
    turn = (wave * x_cell) & (WAVES - 1)
    u = (turn.astype(F32) - WAVES / 2) * (2.0 / WAVES)
    size = jnp.abs(u)
    cos = -sin_pi(0.5 - size)
    sin = sin_pi(jnp.minimum(size, 1.0 - size))
    sin = jnp.where(u < 0, sin, -sin)
    for p in range(POLS):
        re, im = sent[2 * p], sent[2 * p + 1]
        rows_ref[:, 2 * p] = re * cos + im * sin
        rows_ref[:, 2 * p + 1] = im * cos - re * sin
    y_ids = lax.broadcasted_iota(jnp.int32, (CELLS, CELLS), 0).astype(BF16)
    one, zero = jnp.ones((CELLS, CELLS), BF16), jnp.zeros((CELLS, CELLS), BF16)
    y_cells = (cell & (CELLS - 1)).astype(BF16)
    for j in range(LAYERS):
        spot = jnp.where(y_ids == y_cells[j], one, zero)
        values = rows_ref[j].reshape(4 * ROWS, CELLS)
        high = values.astype(BF16)
        low = (values - high.astype(F32)).astype(BF16)
        at_y = lax.dot_general(
            jnp.concatenate([high, low], axis=0), spot, (((1,), (1,)), ((), ())),
            preferred_element_type=F32,
        )
        rows_ref[j] = (at_y[: 4 * ROWS] + at_y[4 * ROWS :]).reshape(4, ROWS, CELLS)
    mix_rows(rows_ref, green_ref, place_ref, table_ref, out_ref, spec_ref, kern_ref, mixed_ref)


def x_inverse(rows_ref, table_ref):
    parts = [
        jnp.concatenate(
            [rows_ref[:, 2 * p + c].reshape(WAVES, CELLS) for p in range(POLS)], axis=1
        )
        for c in range(2)
    ]
    waves = jnp.concatenate(parts, axis=0)
    cells = jnp.dot(thrice(table_ref[...], 1), split_cat(waves, 0), preferred_element_type=F32)
    return [
        [cells[c * CELLS : (c + 1) * CELLS, p * CELLS : (p + 1) * CELLS] for c in range(2)]
        for p in range(POLS)
    ]


def residual_kernel(rows_ref, field_ref, station_ref, seen_ref, error_ref, table_ref, total_ref, sent_ref):
    scattered = x_inverse(rows_ref, table_ref)
    cell = station_ref[...]
    ids = lax.broadcasted_iota(jnp.int32, (CELLS, CELLS), 0)
    x_spot = jnp.where(ids == (cell >> 7), 1.0, 0.0).astype(BF16)
    y_spot = ids == (cell & (CELLS - 1))
    sent = []
    for p in range(POLS):
        weight = error_ref[0, p] * error_ref[0, p]
        for c in range(2):
            total = field_ref[0, p, c, 0] + scattered[p][c]
            total_ref[2 * p + c] = total
            turned = total.T
            picked = jnp.zeros((CELLS, CELLS), F32)
            for _ in range(3):
                piece = turned.astype(BF16)
                picked = picked + jnp.dot(piece, x_spot, preferred_element_type=F32)
                turned = turned - piece.astype(F32)
            predicted = jnp.sum(jnp.where(y_spot, picked, 0.0), axis=0, keepdims=True)
            resid = (predicted - seen_ref[0, p, c]) / weight
            sent.append(-resid if c else resid)
    sent.append(cell.astype(F32))
    message = jnp.concatenate(sent, axis=1)
    sent_ref[...] = jnp.broadcast_to(message[None], (LAYERS, 1, 5 * CELLS))


def gradient_kernel(rows_ref, total_ref, table_ref, out_ref):
    adjoint = x_inverse(rows_ref, table_ref)
    term = jnp.zeros((CELLS, CELLS), F32)
    for p in range(POLS):
        term = term + (total_ref[2 * p] * adjoint[p][0] - total_ref[2 * p + 1] * adjoint[p][1])
    out_ref[...] = jnp.broadcast_to(term[None], (RING, CELLS, CELLS))


def call(kernel, out_shape, scratch=(), smem=0, operands=()):
    specs = [pl.BlockSpec(memory_space=pltpu.SMEM)] * smem
    specs += [pl.BlockSpec(memory_space=pltpu.VMEM)] * (len(operands) - smem)
    if isinstance(out_shape, list):
        out_specs = [pl.BlockSpec(memory_space=pltpu.VMEM)] * len(out_shape)
    else:
        out_specs = pl.BlockSpec(memory_space=pltpu.VMEM)
    return pl.pallas_call(
        kernel,
        out_shape=out_shape,
        in_specs=specs,
        out_specs=out_specs,
        scratch_shapes=list(scratch),
        compiler_params=pltpu.CompilerParams(vmem_limit_bytes=VMEM_BYTES),
    )(*operands)


def over_layers(values):
    return lax.all_to_all(values, "layer", split_axis=0, concat_axis=0, tiled=True)


def sum_over_freq(copies, size):
    rings = [list(range(r, r + RING)) for r in range(0, size, RING)]
    lines = [[r + RING * k for k in (1, 0, 2, 3)] for r in range(RING)]
    for groups in (rings, lines):
        parts = lax.all_to_all(
            copies, "freq", split_axis=0, concat_axis=0, tiled=True, axis_index_groups=groups
        )
        total = (parts[0] + parts[1]) + (parts[2] + parts[3])
        copies = jnp.broadcast_to(total[None], copies.shape)
    return total


def per_device(conductivity, background, green, pair_table, stations, observed, data_error, freqs):
    x_fwd, y_both, x_inv = dft_blocks()
    first = (lax.axis_index("layer") * ROWS).astype(jnp.int32).reshape(1)
    rows_shape = jax.ShapeDtypeStruct((LAYERS, 4, ROWS, CELLS), F32)
    scratch = (
        pltpu.VMEM((2, LAYERS, 3 * POLS * ROWS, CELLS), F32),
        pltpu.VMEM((2, KERNELS, 3 * ROWS, CELLS), F32),
        pltpu.VMEM((POLS, LAYERS, ROWS, 2 * WAVES), F32),
    )
    rows, places = pl.pallas_call(
        x_forward_kernel,
        out_shape=[rows_shape, jax.ShapeDtypeStruct(pair_table.shape, jnp.int32)],
        in_specs=[pl.BlockSpec(memory_space=pl.ANY)] * 5,
        out_specs=[pl.BlockSpec(memory_space=pltpu.VMEM)] * 2,
        scratch_shapes=[
            pltpu.VMEM(conductivity.shape, F32),
            pltpu.VMEM(background.shape, F32),
            pltpu.VMEM(x_fwd.shape, BF16),
            pltpu.VMEM(pair_table.shape, jnp.int32),
            pltpu.SemaphoreType.DMA((4,)),
        ],
        compiler_params=pltpu.CompilerParams(vmem_limit_bytes=FIRST_BYTES),
    )(conductivity, background, x_fwd, pair_table, first)
    back = call(
        mix_kernel, rows_shape, scratch, 1,
        (places, over_layers(rows), green, y_both),
    )
    total, sent = call(
        residual_kernel,
        [
            jax.ShapeDtypeStruct((4, CELLS, CELLS), F32),
            jax.ShapeDtypeStruct((LAYERS, 1, 5 * CELLS), F32),
        ],
        operands=(over_layers(back), background, stations, observed, data_error, x_inv),
    )
    back = call(
        adjoint_mix_kernel, rows_shape,
        (pltpu.VMEM((LAYERS, 4, ROWS, CELLS), F32),) + scratch, 2,
        (places, first, over_layers(sent), green, y_both),
    )
    copies = call(
        gradient_kernel,
        jax.ShapeDtypeStruct((RING, CELLS, CELLS), F32),
        operands=(over_layers(back), total, x_inv),
    )
    return sum_over_freq(copies, freqs)[None]


def solution(mesh):
    in_specs = (
        P("layer", None, None),
        P("freq", None, None, "layer", None, None),
        P("freq", None, None, "layer", None),
        P(),
        P("layer", None),
        P("freq", None, None, "layer", None),
        P("freq", None, "layer", None),
    )
    return jax.shard_map(
        functools.partial(per_device, freqs=mesh.shape["freq"]),
        mesh=mesh, in_specs=in_specs, out_specs=P("layer", None, None), check_vma=False,
    )
```

```python
import functools
import math

import jax
import jax.numpy as jnp
import ml_dtypes
import numpy as np
from jax import lax
from jax.experimental import pallas as pl
from jax.experimental.pallas import tpu as pltpu
from jax.sharding import PartitionSpec as P

CELLS = 128
WAVES = 256
LAYERS = 32
ROWS = 8
KERNELS = 32
POLS = 2
GROUP = 4
STEP = 16
RING = 4
SIN_PI = (0.0776576603, -0.5982912856, 2.5500775232, -5.1677100835, 3.1415926401)
F32 = jnp.float32
BF16 = jnp.bfloat16
VMEM_BYTES = 40 * 1024 * 1024
FIRST_BYTES = 60 * 1024 * 1024


def halves(table):
    high = table.astype(ml_dtypes.bfloat16)
    low = (table - high.astype(np.float64)).astype(ml_dtypes.bfloat16)
    return high, low


def dft_blocks():
    waves = np.arange(WAVES)[:, None]
    cells = np.arange(CELLS)[None, :]
    angles = (waves * cells % WAVES) * (2.0 * math.pi / WAVES)
    cos, sin = np.cos(angles), np.sin(angles)
    x_fwd = np.concatenate([cos, sin], axis=1)
    y_fwd = np.block([[cos.T, -sin.T], [sin.T, cos.T]])
    y_inv = np.block([[cos, sin], [-sin, cos]]) / WAVES
    x_inv = np.block([[cos.T, -sin.T], [sin.T, cos.T]]) / WAVES
    y_both = np.concatenate(
        [np.concatenate(halves(y_fwd), axis=0), np.concatenate(halves(y_inv), axis=1)], axis=0
    )
    return np.concatenate(halves(x_fwd), axis=1), y_both, np.concatenate(halves(x_inv), axis=1)


def thrice(table, axis):
    high, low = jnp.split(table, 2, axis=axis)
    return jnp.concatenate([high, high, low], axis=axis)


def split_cat(values, axis):
    high = values.astype(BF16)
    low = (values - high.astype(F32)).astype(BF16)
    return jnp.concatenate([high, low, high], axis=axis)


def x_forward_kernel(
    cond_hbm, field_hbm, table_hbm, pair_hbm,
    out_ref, place_ref, cond_ref, field_ref, table_ref, pair_ref, sems,
):
    moves = ((field_hbm, field_ref), (cond_hbm, cond_ref), (table_hbm, table_ref), (pair_hbm, pair_ref))
    copies = [
        pltpu.make_async_copy(source, target, sems.at[n])
        for n, (source, target) in enumerate(moves)
    ]
    for copy in copies:
        copy.start()
    copies[0].wait()
    copies[1].wait()
    cond = cond_ref[0]
    high, low = [], []
    for c in range(2):
        part = jnp.concatenate([cond * field_ref[0, p, c, 0] for p in range(POLS)], axis=1)
        high.append(part.astype(BF16))
        low.append((part - high[c].astype(F32)).astype(BF16))
    stacks = [
        jnp.concatenate([jnp.concatenate([part[0], part[1]], axis=1), jnp.concatenate([part[1], -part[0]], axis=1)], axis=0)
        for part in (high, low)
    ]
    cells = jnp.concatenate([stacks[0], stacks[1], stacks[0]], axis=0)
    copies[3].wait()
    place_ref[...] = pair_ref[...] * (3 * ROWS)
    copies[2].wait()
    rows = jnp.dot(thrice(table_ref[...], 1), cells, preferred_element_type=F32)
    for c in range(2):
        for p in range(POLS):
            at = (c * POLS + p) * CELLS
            out_ref[:, 2 * p + c] = rows[:, at : at + CELLS].reshape(LAYERS, ROWS, CELLS)


def mix_rows(rows_ref, green_ref, place_ref, places, table_ref, out_ref, spec_ref, kern_ref, mixed_ref):
    lanes = [slice(h * CELLS, (h + 1) * CELLS) for h in range(2)]
    forward = thrice(table_ref[: 2 * WAVES], 0)
    for p in range(POLS):
        flat = [rows_ref[:, 2 * p + c].reshape(LAYERS * ROWS, CELLS) for c in range(2)]
        both = jnp.concatenate(flat, axis=1)
        spec = jnp.dot(split_cat(both, 1), forward, preferred_element_type=F32)
        h = p
        g_re = green_ref[0, 0, :, :, lanes[h]]
        g_im = green_ref[0, 1, :, :, lanes[h]]
        kern_ref[h, :, 0:ROWS] = g_re + g_im
        kern_ref[h, :, ROWS : 2 * ROWS] = g_re
        kern_ref[h, :, 2 * ROWS :] = g_im
        for h in range(2):
            re = spec[:, h * CELLS : (h + 1) * CELLS].reshape(LAYERS, ROWS, CELLS)
            im = spec[:, WAVES + h * CELLS : WAVES + (h + 1) * CELLS].reshape(LAYERS, ROWS, CELLS)
            for k, value in enumerate((re, im - re, re + im)):
                at = (3 * p + k) * ROWS
                spec_ref[h, :, at : at + ROWS] = value

    places.wait()
    kern = [kern_ref.at[h].reshape(KERNELS * 3 * ROWS, CELLS) for h in range(2)]
    for h in range(2):

        def one_group(group, carry, h=h):
            first = group * GROUP

            def some_sources(chunk, sums):
                sums = list(sums)
                for s in range(STEP):
                    j = chunk * STEP + s
                    src = [spec_ref[h, j, k * ROWS : (k + 1) * ROWS] for k in range(3 * POLS)]
                    for r in range(GROUP):
                        place = place_ref[first + r, j]
                        for k in range(3):
                            row = pl.multiple_of(place + k * ROWS, ROWS)
                            factor = kern[h][pl.ds(row, ROWS), :]
                            for p in range(POLS):
                                at = (r * POLS + p) * 3 + k
                                sums[at] = sums[at] + factor * src[3 * p + k]
                return tuple(sums)

            zero = jnp.zeros((ROWS, CELLS), F32)
            sums = lax.fori_loop(
                0, LAYERS // STEP, some_sources, (zero,) * (GROUP * POLS * 3)
            )
            for r in range(GROUP):
                for p in range(POLS):
                    one, two, three = sums[(r * POLS + p) * 3 : (r * POLS + p) * 3 + 3]
                    mixed_ref[p, first + r, :, h * CELLS : (h + 1) * CELLS] = one - three
                    mixed_ref[p, first + r, :, WAVES + h * CELLS : WAVES + (h + 1) * CELLS] = one + two
            return carry

        lax.fori_loop(0, LAYERS // GROUP, one_group, 0)

    high, low = table_ref[2 * WAVES :, :WAVES], table_ref[2 * WAVES :, WAVES:]
    inverse = jnp.concatenate([high, high, low], axis=0)
    for p in range(POLS):
        mixed = mixed_ref[p].reshape(LAYERS * ROWS, 2 * WAVES)
        back = jnp.dot(split_cat(mixed, 1), inverse, preferred_element_type=F32)
        for c in range(2):
            out_ref[:, 2 * p + c] = back[:, c * CELLS : (c + 1) * CELLS].reshape(LAYERS, ROWS, CELLS)


def mix_kernel(
    place_any, rows_ref, green_ref, table_ref, out_ref, spec_ref, kern_ref, mixed_ref, place_ref, sem
):
    places = pltpu.make_async_copy(place_any, place_ref, sem)
    places.start()
    mix_rows(rows_ref, green_ref, place_ref, places, table_ref, out_ref, spec_ref, kern_ref, mixed_ref)


def sin_pi(v):
    square = v * v
    total = jnp.full_like(v, SIN_PI[0])
    for factor in SIN_PI[1:]:
        total = total * square + factor
    return total * v


def adjoint_mix_kernel(
    place_any, sent_ref, green_ref, table_ref,
    out_ref, rows_ref, spec_ref, kern_ref, mixed_ref, place_ref, sem,
):
    places = pltpu.make_async_copy(place_any, place_ref, sem)
    places.start()
    sent = [sent_ref[:, :, k * CELLS : (k + 1) * CELLS] for k in range(5)]
    cell = sent[4].astype(jnp.int32)
    x_cell = cell >> 7
    wave = lax.axis_index("layer") * ROWS + lax.broadcasted_iota(jnp.int32, (LAYERS, ROWS, CELLS), 1)
    turn = (wave * x_cell) & (WAVES - 1)
    u = (turn.astype(F32) - WAVES / 2) * (2.0 / WAVES)
    size = jnp.abs(u)
    cos = -sin_pi(0.5 - size)
    sin = sin_pi(jnp.minimum(size, 1.0 - size))
    sin = jnp.where(u < 0, sin, -sin)
    for p in range(POLS):
        re, im = sent[2 * p], sent[2 * p + 1]
        rows_ref[:, 2 * p] = re * cos + im * sin
        rows_ref[:, 2 * p + 1] = im * cos - re * sin
    y_ids = lax.broadcasted_iota(jnp.int32, (CELLS, CELLS), 0).astype(BF16)
    one, zero = jnp.ones((CELLS, CELLS), BF16), jnp.zeros((CELLS, CELLS), BF16)
    y_cells = (cell & (CELLS - 1)).astype(BF16)
    for j in range(LAYERS):
        spot = jnp.where(y_ids == y_cells[j], one, zero)
        values = rows_ref[j].reshape(4 * ROWS, CELLS)
        high = values.astype(BF16)
        low = (values - high.astype(F32)).astype(BF16)
        at_y = lax.dot_general(
            jnp.concatenate([high, low], axis=0), spot, (((1,), (1,)), ((), ())),
            preferred_element_type=F32,
        )
        rows_ref[j] = (at_y[: 4 * ROWS] + at_y[4 * ROWS :]).reshape(4, ROWS, CELLS)
    mix_rows(rows_ref, green_ref, place_ref, places, table_ref, out_ref, spec_ref, kern_ref, mixed_ref)


def x_inverse(rows_ref, table_ref):
    parts = [
        jnp.concatenate(
            [rows_ref[:, 2 * p + c].reshape(WAVES, CELLS) for p in range(POLS)], axis=1
        )
        for c in range(2)
    ]
    waves = jnp.concatenate(parts, axis=0)
    cells = jnp.dot(thrice(table_ref[...], 1), split_cat(waves, 0), preferred_element_type=F32)
    return [
        [cells[c * CELLS : (c + 1) * CELLS, p * CELLS : (p + 1) * CELLS] for c in range(2)]
        for p in range(POLS)
    ]


def residual_kernel(rows_ref, field_ref, station_ref, seen_ref, error_ref, table_ref, total_ref, sent_ref):
    scattered = x_inverse(rows_ref, table_ref)
    cell = station_ref[...]
    ids = lax.broadcasted_iota(jnp.int32, (CELLS, CELLS), 0)
    x_spot = jnp.where(ids == (cell >> 7), 1.0, 0.0).astype(BF16)
    y_spot = ids == (cell & (CELLS - 1))
    sent = []
    for p in range(POLS):
        weight = error_ref[0, p] * error_ref[0, p]
        for c in range(2):
            total = field_ref[0, p, c, 0] + scattered[p][c]
            total_ref[2 * p + c] = total
            turned = total.T
            picked = jnp.zeros((CELLS, CELLS), F32)
            for _ in range(3):
                piece = turned.astype(BF16)
                picked = picked + jnp.dot(piece, x_spot, preferred_element_type=F32)
                turned = turned - piece.astype(F32)
            predicted = jnp.sum(jnp.where(y_spot, picked, 0.0), axis=0, keepdims=True)
            resid = (predicted - seen_ref[0, p, c]) / weight
            sent.append(-resid if c else resid)
    sent.append(cell.astype(F32))
    message = jnp.concatenate(sent, axis=1)
    sent_ref[...] = jnp.broadcast_to(message[None], (LAYERS, 1, 5 * CELLS))


def gradient_kernel(rows_ref, total_ref, table_ref, out_ref):
    adjoint = x_inverse(rows_ref, table_ref)
    term = jnp.zeros((CELLS, CELLS), F32)
    for p in range(POLS):
        term = term + (total_ref[2 * p] * adjoint[p][0] - total_ref[2 * p + 1] * adjoint[p][1])
    out_ref[...] = jnp.broadcast_to(term[None], (RING, CELLS, CELLS))


def call(kernel, out_shape, scratch=(), loose=0, operands=()):
    specs = [pl.BlockSpec(memory_space=pl.ANY)] * loose
    specs += [pl.BlockSpec(memory_space=pltpu.VMEM)] * (len(operands) - loose)
    if isinstance(out_shape, list):
        out_specs = [pl.BlockSpec(memory_space=pltpu.VMEM)] * len(out_shape)
    else:
        out_specs = pl.BlockSpec(memory_space=pltpu.VMEM)
    return pl.pallas_call(
        kernel,
        out_shape=out_shape,
        in_specs=specs,
        out_specs=out_specs,
        scratch_shapes=list(scratch),
        compiler_params=pltpu.CompilerParams(vmem_limit_bytes=VMEM_BYTES),
    )(*operands)


def over_layers(values):
    return lax.all_to_all(values, "layer", split_axis=0, concat_axis=0, tiled=True)


def sum_over_freq(copies, size):
    rings = [list(range(r, r + RING)) for r in range(0, size, RING)]
    lines = [[r + RING * k for k in (1, 0, 2, 3)] for r in range(RING)]
    for groups in (rings, lines):
        parts = lax.all_to_all(
            copies, "freq", split_axis=0, concat_axis=0, tiled=True, axis_index_groups=groups
        )
        total = (parts[0] + parts[1]) + (parts[2] + parts[3])
        copies = jnp.broadcast_to(total[None], copies.shape)
    return total


def per_device(conductivity, background, green, pair_table, stations, observed, data_error, freqs):
    x_fwd, y_both, x_inv = dft_blocks()
    rows_shape = jax.ShapeDtypeStruct((LAYERS, 4, ROWS, CELLS), F32)
    scratch = (
        pltpu.VMEM((2, LAYERS, 3 * POLS * ROWS, CELLS), F32),
        pltpu.VMEM((2, KERNELS, 3 * ROWS, CELLS), F32),
        pltpu.VMEM((POLS, LAYERS, ROWS, 2 * WAVES), F32),
        pltpu.SMEM(pair_table.shape, jnp.int32),
        pltpu.SemaphoreType.DMA(()),
    )
    rows, places = pl.pallas_call(
        x_forward_kernel,
        out_shape=[rows_shape, jax.ShapeDtypeStruct(pair_table.shape, jnp.int32)],
        in_specs=[pl.BlockSpec(memory_space=pl.ANY)] * 4,
        out_specs=[pl.BlockSpec(memory_space=pltpu.VMEM)] * 2,
        scratch_shapes=[
            pltpu.VMEM(conductivity.shape, F32),
            pltpu.VMEM(background.shape, F32),
            pltpu.VMEM(x_fwd.shape, BF16),
            pltpu.VMEM(pair_table.shape, jnp.int32),
            pltpu.SemaphoreType.DMA((4,)),
        ],
        compiler_params=pltpu.CompilerParams(vmem_limit_bytes=FIRST_BYTES),
    )(conductivity, background, x_fwd, pair_table)
    back = call(
        mix_kernel, rows_shape, scratch, 1,
        (places, over_layers(rows), green, y_both),
    )
    total, sent = call(
        residual_kernel,
        [
            jax.ShapeDtypeStruct((4, CELLS, CELLS), F32),
            jax.ShapeDtypeStruct((LAYERS, 1, 5 * CELLS), F32),
        ],
        operands=(over_layers(back), background, stations, observed, data_error, x_inv),
    )
    back = call(
        adjoint_mix_kernel, rows_shape,
        (pltpu.VMEM((LAYERS, 4, ROWS, CELLS), F32),) + scratch, 1,
        (places, over_layers(sent), green, y_both),
    )
    copies = call(
        gradient_kernel,
        jax.ShapeDtypeStruct((RING, CELLS, CELLS), F32),
        operands=(over_layers(back), total, x_inv),
    )
    return sum_over_freq(copies, freqs)[None]


def solution(mesh):
    in_specs = (
        P("layer", None, None),
        P("freq", None, None, "layer", None, None),
        P("freq", None, None, "layer", None),
        P(),
        P("layer", None),
        P("freq", None, None, "layer", None),
        P("freq", None, "layer", None),
    )
    return jax.shard_map(
        functools.partial(per_device, freqs=mesh.shape["freq"]),
        mesh=mesh, in_specs=in_specs, out_specs=P("layer", None, None), check_vma=False,
    )
```

```python
import functools
import math

import jax
import jax.numpy as jnp
import ml_dtypes
import numpy as np
from jax import lax
from jax.experimental import pallas as pl
from jax.experimental.pallas import tpu as pltpu
from jax.sharding import PartitionSpec as P

CELLS = 128
WAVES = 256
LAYERS = 32
ROWS = 8
KERNELS = 32
POLS = 2
GROUP = 4
STEP = 16
RING = 4
LEAD = 24
SIN_PI = (0.0776576603, -0.5982912856, 2.5500775232, -5.1677100835, 3.1415926401)
F32 = jnp.float32
BF16 = jnp.bfloat16
VMEM_BYTES = 40 * 1024 * 1024
FIRST_BYTES = 60 * 1024 * 1024


def halves(table):
    high = table.astype(ml_dtypes.bfloat16)
    low = (table - high.astype(np.float64)).astype(ml_dtypes.bfloat16)
    return high, low


def dft_blocks():
    waves = np.arange(WAVES)[:, None]
    cells = np.arange(CELLS)[None, :]
    angles = (waves * cells % WAVES) * (2.0 * math.pi / WAVES)
    cos, sin = np.cos(angles), np.sin(angles)
    parts = np.arange(WAVES).reshape(LAYERS, ROWS)[np.arange(LAYERS) ^ LEAD].reshape(-1)
    x_fwd = np.concatenate([cos, sin], axis=1)[parts]
    y_fwd = np.block([[cos.T, -sin.T], [sin.T, cos.T]])
    y_inv = np.block([[cos, sin], [-sin, cos]]) / WAVES
    x_inv = np.block([[cos[parts].T, -sin[parts].T], [sin[parts].T, cos[parts].T]]) / WAVES
    y_both = np.concatenate(
        [np.concatenate(halves(y_fwd), axis=0), np.concatenate(halves(y_inv), axis=1)], axis=0
    )
    return np.concatenate(halves(x_fwd), axis=1), y_both, np.concatenate(halves(x_inv), axis=1)


def thrice(table, axis):
    high, low = jnp.split(table, 2, axis=axis)
    return jnp.concatenate([high, high, low], axis=axis)


def split_cat(values, axis):
    high = values.astype(BF16)
    low = (values - high.astype(F32)).astype(BF16)
    return jnp.concatenate([high, low, high], axis=axis)


def x_forward_kernel(
    cond_hbm, field_hbm, table_hbm, pair_hbm,
    out_ref, place_ref, cond_ref, field_ref, table_ref, pair_ref, sems,
):
    moves = ((field_hbm, field_ref), (cond_hbm, cond_ref), (table_hbm, table_ref), (pair_hbm, pair_ref))
    copies = [
        pltpu.make_async_copy(source, target, sems.at[n])
        for n, (source, target) in enumerate(moves)
    ]
    for copy in copies:
        copy.start()
    copies[0].wait()
    copies[1].wait()
    cond = cond_ref[0]
    high, low = [], []
    for c in range(2):
        part = jnp.concatenate([cond * field_ref[0, p, c, 0] for p in range(POLS)], axis=1)
        high.append(part.astype(BF16))
        low.append((part - high[c].astype(F32)).astype(BF16))
    stacks = [
        jnp.concatenate([jnp.concatenate([part[0], part[1]], axis=1), jnp.concatenate([part[1], -part[0]], axis=1)], axis=0)
        for part in (high, low)
    ]
    cells = jnp.concatenate([stacks[0], stacks[1], stacks[0]], axis=0)
    copies[3].wait()
    place_ref[...] = pair_ref[...] * (3 * ROWS)
    copies[2].wait()
    rows = jnp.dot(thrice(table_ref[...], 1), cells, preferred_element_type=F32)
    for c in range(2):
        for p in range(POLS):
            at = (c * POLS + p) * CELLS
            out_ref[:, 2 * p + c] = rows[:, at : at + CELLS].reshape(LAYERS, ROWS, CELLS)


def mix_rows(rows_ref, green_ref, place_ref, places, table_ref, out_ref, spec_ref, kern_ref, mixed_ref):
    lanes = [slice(h * CELLS, (h + 1) * CELLS) for h in range(2)]
    forward = thrice(table_ref[: 2 * WAVES], 0)
    for p in range(POLS):
        flat = [rows_ref[:, 2 * p + c].reshape(LAYERS * ROWS, CELLS) for c in range(2)]
        both = jnp.concatenate(flat, axis=1)
        spec = jnp.dot(split_cat(both, 1), forward, preferred_element_type=F32)
        h = p
        g_re = green_ref[0, 0, :, :, lanes[h]]
        g_im = green_ref[0, 1, :, :, lanes[h]]
        kern_ref[h, :, 0:ROWS] = g_re + g_im
        kern_ref[h, :, ROWS : 2 * ROWS] = g_re
        kern_ref[h, :, 2 * ROWS :] = g_im
        for h in range(2):
            re = spec[:, h * CELLS : (h + 1) * CELLS].reshape(LAYERS, ROWS, CELLS)
            im = spec[:, WAVES + h * CELLS : WAVES + (h + 1) * CELLS].reshape(LAYERS, ROWS, CELLS)
            for k, value in enumerate((re, im - re, re + im)):
                at = (3 * p + k) * ROWS
                spec_ref[h, :, at : at + ROWS] = value

    places.wait()
    kern = [kern_ref.at[h].reshape(KERNELS * 3 * ROWS, CELLS) for h in range(2)]
    for h in range(2):

        def one_group(group, carry, h=h):
            first = group * GROUP
            first_layer = (group ^ (LEAD // GROUP)) * GROUP

            def some_sources(chunk, sums):
                sums = list(sums)
                for s in range(STEP):
                    j = chunk * STEP + s
                    src = [spec_ref[h, j, k * ROWS : (k + 1) * ROWS] for k in range(3 * POLS)]
                    layer = (chunk ^ (LEAD // STEP)) * STEP + (s ^ (LEAD % STEP))
                    for r in range(GROUP):
                        place = place_ref[first_layer + r, layer]
                        for k in range(3):
                            row = pl.multiple_of(place + k * ROWS, ROWS)
                            factor = kern[h][pl.ds(row, ROWS), :]
                            for p in range(POLS):
                                at = (r * POLS + p) * 3 + k
                                sums[at] = sums[at] + factor * src[3 * p + k]
                return tuple(sums)

            zero = jnp.zeros((ROWS, CELLS), F32)
            sums = lax.fori_loop(
                0, LAYERS // STEP, some_sources, (zero,) * (GROUP * POLS * 3)
            )
            for r in range(GROUP):
                for p in range(POLS):
                    one, two, three = sums[(r * POLS + p) * 3 : (r * POLS + p) * 3 + 3]
                    mixed_ref[p, first + r, :, h * CELLS : (h + 1) * CELLS] = one - three
                    mixed_ref[p, first + r, :, WAVES + h * CELLS : WAVES + (h + 1) * CELLS] = one + two
            return carry

        lax.fori_loop(0, LAYERS // GROUP, one_group, 0)

    high, low = table_ref[2 * WAVES :, :WAVES], table_ref[2 * WAVES :, WAVES:]
    inverse = jnp.concatenate([high, high, low], axis=0)
    for p in range(POLS):
        mixed = mixed_ref[p].reshape(LAYERS * ROWS, 2 * WAVES)
        back = jnp.dot(split_cat(mixed, 1), inverse, preferred_element_type=F32)
        for c in range(2):
            out_ref[:, 2 * p + c] = back[:, c * CELLS : (c + 1) * CELLS].reshape(LAYERS, ROWS, CELLS)


def mix_kernel(
    place_any, rows_ref, green_ref, table_ref, out_ref, spec_ref, kern_ref, mixed_ref, place_ref, sem
):
    places = pltpu.make_async_copy(place_any, place_ref, sem)
    places.start()
    mix_rows(rows_ref, green_ref, place_ref, places, table_ref, out_ref, spec_ref, kern_ref, mixed_ref)


def sin_pi(v):
    square = v * v
    total = jnp.full_like(v, SIN_PI[0])
    for factor in SIN_PI[1:]:
        total = total * square + factor
    return total * v


def adjoint_mix_kernel(
    place_any, sent_ref, green_ref, table_ref,
    out_ref, rows_ref, spec_ref, kern_ref, mixed_ref, place_ref, sem,
):
    places = pltpu.make_async_copy(place_any, place_ref, sem)
    places.start()
    sent = [sent_ref[:, :, k * CELLS : (k + 1) * CELLS] for k in range(5)]
    cell = sent[4].astype(jnp.int32)
    x_cell = cell >> 7
    wave = lax.axis_index("layer") * ROWS + lax.broadcasted_iota(jnp.int32, (LAYERS, ROWS, CELLS), 1)
    turn = (wave * x_cell) & (WAVES - 1)
    u = (turn.astype(F32) - WAVES / 2) * (2.0 / WAVES)
    size = jnp.abs(u)
    cos = -sin_pi(0.5 - size)
    sin = sin_pi(jnp.minimum(size, 1.0 - size))
    sin = jnp.where(u < 0, sin, -sin)
    for p in range(POLS):
        re, im = sent[2 * p], sent[2 * p + 1]
        rows_ref[:, 2 * p] = re * cos + im * sin
        rows_ref[:, 2 * p + 1] = im * cos - re * sin
    y_ids = lax.broadcasted_iota(jnp.int32, (CELLS, CELLS), 0).astype(BF16)
    one, zero = jnp.ones((CELLS, CELLS), BF16), jnp.zeros((CELLS, CELLS), BF16)
    y_cells = (cell & (CELLS - 1)).astype(BF16)
    for j in range(LAYERS):
        spot = jnp.where(y_ids == y_cells[j], one, zero)
        values = rows_ref[j].reshape(4 * ROWS, CELLS)
        high = values.astype(BF16)
        low = (values - high.astype(F32)).astype(BF16)
        at_y = lax.dot_general(
            jnp.concatenate([high, low], axis=0), spot, (((1,), (1,)), ((), ())),
            preferred_element_type=F32,
        )
        rows_ref[j] = (at_y[: 4 * ROWS] + at_y[4 * ROWS :]).reshape(4, ROWS, CELLS)
    mix_rows(rows_ref, green_ref, place_ref, places, table_ref, out_ref, spec_ref, kern_ref, mixed_ref)


def x_inverse(rows_ref, table_ref):
    parts = [
        jnp.concatenate(
            [rows_ref[:, 2 * p + c].reshape(WAVES, CELLS) for p in range(POLS)], axis=1
        )
        for c in range(2)
    ]
    waves = jnp.concatenate(parts, axis=0)
    cells = jnp.dot(thrice(table_ref[...], 1), split_cat(waves, 0), preferred_element_type=F32)
    return [
        [cells[c * CELLS : (c + 1) * CELLS, p * CELLS : (p + 1) * CELLS] for c in range(2)]
        for p in range(POLS)
    ]


def residual_kernel(rows_ref, field_ref, station_ref, seen_ref, error_ref, table_ref, total_ref, sent_ref):
    scattered = x_inverse(rows_ref, table_ref)
    cell = station_ref[...]
    ids = lax.broadcasted_iota(jnp.int32, (CELLS, CELLS), 0)
    x_spot = jnp.where(ids == (cell >> 7), 1.0, 0.0).astype(BF16)
    y_spot = ids == (cell & (CELLS - 1))
    sent = []
    for p in range(POLS):
        weight = error_ref[0, p] * error_ref[0, p]
        for c in range(2):
            total = field_ref[0, p, c, 0] + scattered[p][c]
            total_ref[2 * p + c] = total
            turned = total.T
            picked = jnp.zeros((CELLS, CELLS), F32)
            for _ in range(3):
                piece = turned.astype(BF16)
                picked = picked + jnp.dot(piece, x_spot, preferred_element_type=F32)
                turned = turned - piece.astype(F32)
            predicted = jnp.sum(jnp.where(y_spot, picked, 0.0), axis=0, keepdims=True)
            resid = (predicted - seen_ref[0, p, c]) / weight
            sent.append(-resid if c else resid)
    sent.append(cell.astype(F32))
    message = jnp.concatenate(sent, axis=1)
    sent_ref[...] = jnp.broadcast_to(message[None], (LAYERS, 1, 5 * CELLS))


def gradient_kernel(rows_ref, total_ref, table_ref, out_ref):
    adjoint = x_inverse(rows_ref, table_ref)
    term = jnp.zeros((CELLS, CELLS), F32)
    for p in range(POLS):
        term = term + (total_ref[2 * p] * adjoint[p][0] - total_ref[2 * p + 1] * adjoint[p][1])
    out_ref[...] = jnp.broadcast_to(term[None], (RING, CELLS, CELLS))


def call(kernel, out_shape, scratch=(), loose=0, operands=()):
    specs = [pl.BlockSpec(memory_space=pl.ANY)] * loose
    specs += [pl.BlockSpec(memory_space=pltpu.VMEM)] * (len(operands) - loose)
    if isinstance(out_shape, list):
        out_specs = [pl.BlockSpec(memory_space=pltpu.VMEM)] * len(out_shape)
    else:
        out_specs = pl.BlockSpec(memory_space=pltpu.VMEM)
    return pl.pallas_call(
        kernel,
        out_shape=out_shape,
        in_specs=specs,
        out_specs=out_specs,
        scratch_shapes=list(scratch),
        compiler_params=pltpu.CompilerParams(vmem_limit_bytes=VMEM_BYTES),
    )(*operands)


def over_layers(values):
    groups = [[k ^ LEAD for k in range(LAYERS)]]
    return lax.all_to_all(
        values, "layer", split_axis=0, concat_axis=0, tiled=True, axis_index_groups=groups
    )


def sum_over_freq(copies, size):
    rings = [list(range(r, r + RING)) for r in range(0, size, RING)]
    lines = [[r + RING * k for k in (2, 1, 0, 3)] for r in range(RING)]
    for groups in (rings, lines):
        parts = lax.all_to_all(
            copies, "freq", split_axis=0, concat_axis=0, tiled=True, axis_index_groups=groups
        )
        total = (parts[0] + parts[1]) + (parts[2] + parts[3])
        copies = jnp.broadcast_to(total[None], copies.shape)
    return total


def per_device(conductivity, background, green, pair_table, stations, observed, data_error, freqs):
    x_fwd, y_both, x_inv = dft_blocks()
    rows_shape = jax.ShapeDtypeStruct((LAYERS, 4, ROWS, CELLS), F32)
    scratch = (
        pltpu.VMEM((2, LAYERS, 3 * POLS * ROWS, CELLS), F32),
        pltpu.VMEM((2, KERNELS, 3 * ROWS, CELLS), F32),
        pltpu.VMEM((POLS, LAYERS, ROWS, 2 * WAVES), F32),
        pltpu.SMEM(pair_table.shape, jnp.int32),
        pltpu.SemaphoreType.DMA(()),
    )
    rows, places = pl.pallas_call(
        x_forward_kernel,
        out_shape=[rows_shape, jax.ShapeDtypeStruct(pair_table.shape, jnp.int32)],
        in_specs=[pl.BlockSpec(memory_space=pl.ANY)] * 4,
        out_specs=[pl.BlockSpec(memory_space=pltpu.VMEM)] * 2,
        scratch_shapes=[
            pltpu.VMEM(conductivity.shape, F32),
            pltpu.VMEM(background.shape, F32),
            pltpu.VMEM(x_fwd.shape, BF16),
            pltpu.VMEM(pair_table.shape, jnp.int32),
            pltpu.SemaphoreType.DMA((4,)),
        ],
        compiler_params=pltpu.CompilerParams(vmem_limit_bytes=FIRST_BYTES),
    )(conductivity, background, x_fwd, pair_table)
    back = call(
        mix_kernel, rows_shape, scratch, 1,
        (places, over_layers(rows), green, y_both),
    )
    total, sent = call(
        residual_kernel,
        [
            jax.ShapeDtypeStruct((4, CELLS, CELLS), F32),
            jax.ShapeDtypeStruct((LAYERS, 1, 5 * CELLS), F32),
        ],
        operands=(over_layers(back), background, stations, observed, data_error, x_inv),
    )
    back = call(
        adjoint_mix_kernel, rows_shape,
        (pltpu.VMEM((LAYERS, 4, ROWS, CELLS), F32),) + scratch, 1,
        (places, over_layers(sent), green, y_both),
    )
    copies = call(
        gradient_kernel,
        jax.ShapeDtypeStruct((RING, CELLS, CELLS), F32),
        operands=(over_layers(back), total, x_inv),
    )
    return sum_over_freq(copies, freqs)[None]


def solution(mesh):
    in_specs = (
        P("layer", None, None),
        P("freq", None, None, "layer", None, None),
        P("freq", None, None, "layer", None),
        P(),
        P("layer", None),
        P("freq", None, None, "layer", None),
        P("freq", None, "layer", None),
    )
    return jax.shard_map(
        functools.partial(per_device, freqs=mesh.shape["freq"]),
        mesh=mesh, in_specs=in_specs, out_specs=P("layer", None, None), check_vma=False,
    )
```

```python
import functools
import math

import jax
import jax.numpy as jnp
import ml_dtypes
import numpy as np
from jax import lax
from jax.experimental import pallas as pl
from jax.experimental.pallas import tpu as pltpu
from jax.sharding import PartitionSpec as P

CELLS = 128
WAVES = 256
LAYERS = 32
ROWS = 8
KERNELS = 32
POLS = 2
GROUP = 4
STEP = 16
RING = 4
LEAD = 27
SIN_PI = (0.0776576603, -0.5982912856, 2.5500775232, -5.1677100835, 3.1415926401)
F32 = jnp.float32
BF16 = jnp.bfloat16
VMEM_BYTES = 40 * 1024 * 1024
FIRST_BYTES = 60 * 1024 * 1024


def halves(table):
    high = table.astype(ml_dtypes.bfloat16)
    low = (table - high.astype(np.float64)).astype(ml_dtypes.bfloat16)
    return high, low


def dft_blocks():
    waves = np.arange(WAVES)[:, None]
    cells = np.arange(CELLS)[None, :]
    angles = (waves * cells % WAVES) * (2.0 * math.pi / WAVES)
    cos, sin = np.cos(angles), np.sin(angles)
    parts = np.arange(WAVES).reshape(LAYERS, ROWS)[np.arange(LAYERS) ^ LEAD].reshape(-1)
    x_fwd = np.concatenate([cos, sin], axis=1)[parts]
    y_fwd = np.block([[cos.T, -sin.T], [sin.T, cos.T]])
    y_inv = np.block([[cos, sin], [-sin, cos]]) / WAVES
    x_inv = np.block([[cos[parts].T, -sin[parts].T], [sin[parts].T, cos[parts].T]]) / WAVES
    y_both = np.concatenate(
        [np.concatenate(halves(y_fwd), axis=0), np.concatenate(halves(y_inv), axis=1)], axis=0
    )
    return np.concatenate(halves(x_fwd), axis=1), y_both, np.concatenate(halves(x_inv), axis=1)


def thrice(table, axis):
    high, low = jnp.split(table, 2, axis=axis)
    return jnp.concatenate([high, high, low], axis=axis)


def split_cat(values, axis):
    high = values.astype(BF16)
    low = (values - high.astype(F32)).astype(BF16)
    return jnp.concatenate([high, low, high], axis=axis)


def x_forward_kernel(
    cond_hbm, field_hbm, table_hbm, pair_hbm,
    out_ref, place_ref, cond_ref, field_ref, table_ref, pair_ref, sems,
):
    moves = ((field_hbm, field_ref), (cond_hbm, cond_ref), (table_hbm, table_ref), (pair_hbm, pair_ref))
    copies = [
        pltpu.make_async_copy(source, target, sems.at[n])
        for n, (source, target) in enumerate(moves)
    ]
    for copy in copies:
        copy.start()
    copies[0].wait()
    copies[1].wait()
    cond = cond_ref[0]
    high, low = [], []
    for c in range(2):
        part = jnp.concatenate([cond * field_ref[0, p, c, 0] for p in range(POLS)], axis=1)
        high.append(part.astype(BF16))
        low.append((part - high[c].astype(F32)).astype(BF16))
    stacks = [
        jnp.concatenate([jnp.concatenate([part[0], part[1]], axis=1), jnp.concatenate([part[1], -part[0]], axis=1)], axis=0)
        for part in (high, low)
    ]
    cells = jnp.concatenate([stacks[0], stacks[1], stacks[0]], axis=0)
    copies[3].wait()
    place_ref[...] = pair_ref[...] * (3 * ROWS)
    copies[2].wait()
    rows = jnp.dot(thrice(table_ref[...], 1), cells, preferred_element_type=F32)
    for c in range(2):
        for p in range(POLS):
            at = (c * POLS + p) * CELLS
            out_ref[:, 2 * p + c] = rows[:, at : at + CELLS].reshape(LAYERS, ROWS, CELLS)


def mix_rows(rows_ref, green_ref, place_ref, places, table_ref, out_ref, spec_ref, kern_ref, mixed_ref):
    lanes = [slice(h * CELLS, (h + 1) * CELLS) for h in range(2)]
    forward = thrice(table_ref[: 2 * WAVES], 0)
    for p in range(POLS):
        flat = [rows_ref[:, 2 * p + c].reshape(LAYERS * ROWS, CELLS) for c in range(2)]
        both = jnp.concatenate(flat, axis=1)
        spec = jnp.dot(split_cat(both, 1), forward, preferred_element_type=F32)
        h = p
        g_re = green_ref[0, 0, :, :, lanes[h]]
        g_im = green_ref[0, 1, :, :, lanes[h]]
        kern_ref[h, :, 0:ROWS] = g_re + g_im
        kern_ref[h, :, ROWS : 2 * ROWS] = g_re
        kern_ref[h, :, 2 * ROWS :] = g_im
        for h in range(2):
            re = spec[:, h * CELLS : (h + 1) * CELLS].reshape(LAYERS, ROWS, CELLS)
            im = spec[:, WAVES + h * CELLS : WAVES + (h + 1) * CELLS].reshape(LAYERS, ROWS, CELLS)
            for k, value in enumerate((re, im - re, re + im)):
                at = (3 * p + k) * ROWS
                spec_ref[h, :, at : at + ROWS] = value

    places.wait()
    kern = [kern_ref.at[h].reshape(KERNELS * 3 * ROWS, CELLS) for h in range(2)]
    for h in range(2):

        def one_group(group, carry, h=h):
            first = group * GROUP
            first_layer = (group ^ (LEAD // GROUP)) * GROUP

            def some_sources(chunk, sums):
                sums = list(sums)
                for s in range(STEP):
                    j = chunk * STEP + s
                    src = [spec_ref[h, j, k * ROWS : (k + 1) * ROWS] for k in range(3 * POLS)]
                    layer = (chunk ^ (LEAD // STEP)) * STEP + (s ^ (LEAD % STEP))
                    for r in range(GROUP):
                        place = place_ref[first_layer + (r ^ (LEAD % GROUP)), layer]
                        for k in range(3):
                            row = pl.multiple_of(place + k * ROWS, ROWS)
                            factor = kern[h][pl.ds(row, ROWS), :]
                            for p in range(POLS):
                                at = (r * POLS + p) * 3 + k
                                sums[at] = sums[at] + factor * src[3 * p + k]
                return tuple(sums)

            zero = jnp.zeros((ROWS, CELLS), F32)
            sums = lax.fori_loop(
                0, LAYERS // STEP, some_sources, (zero,) * (GROUP * POLS * 3)
            )
            for r in range(GROUP):
                for p in range(POLS):
                    one, two, three = sums[(r * POLS + p) * 3 : (r * POLS + p) * 3 + 3]
                    mixed_ref[p, first + r, :, h * CELLS : (h + 1) * CELLS] = one - three
                    mixed_ref[p, first + r, :, WAVES + h * CELLS : WAVES + (h + 1) * CELLS] = one + two
            return carry

        lax.fori_loop(0, LAYERS // GROUP, one_group, 0)

    high, low = table_ref[2 * WAVES :, :WAVES], table_ref[2 * WAVES :, WAVES:]
    inverse = jnp.concatenate([high, high, low], axis=0)
    for p in range(POLS):
        mixed = mixed_ref[p].reshape(LAYERS * ROWS, 2 * WAVES)
        back = jnp.dot(split_cat(mixed, 1), inverse, preferred_element_type=F32)
        for c in range(2):
            out_ref[:, 2 * p + c] = back[:, c * CELLS : (c + 1) * CELLS].reshape(LAYERS, ROWS, CELLS)


def mix_kernel(
    place_any, rows_ref, green_ref, table_ref, out_ref, spec_ref, kern_ref, mixed_ref, place_ref, sem
):
    places = pltpu.make_async_copy(place_any, place_ref, sem)
    places.start()
    mix_rows(rows_ref, green_ref, place_ref, places, table_ref, out_ref, spec_ref, kern_ref, mixed_ref)


def sin_pi(v):
    square = v * v
    total = jnp.full_like(v, SIN_PI[0])
    for factor in SIN_PI[1:]:
        total = total * square + factor
    return total * v


def adjoint_mix_kernel(
    place_any, sent_ref, green_ref, table_ref,
    out_ref, rows_ref, spec_ref, kern_ref, mixed_ref, place_ref, sem,
):
    places = pltpu.make_async_copy(place_any, place_ref, sem)
    places.start()
    sent = [sent_ref[:, :, k * CELLS : (k + 1) * CELLS] for k in range(5)]
    cell = sent[4].astype(jnp.int32)
    x_cell = cell >> 7
    wave = lax.axis_index("layer") * ROWS + lax.broadcasted_iota(jnp.int32, (LAYERS, ROWS, CELLS), 1)
    turn = (wave * x_cell) & (WAVES - 1)
    u = (turn.astype(F32) - WAVES / 2) * (2.0 / WAVES)
    size = jnp.abs(u)
    cos = -sin_pi(0.5 - size)
    sin = sin_pi(jnp.minimum(size, 1.0 - size))
    sin = jnp.where(u < 0, sin, -sin)
    for p in range(POLS):
        re, im = sent[2 * p], sent[2 * p + 1]
        rows_ref[:, 2 * p] = re * cos + im * sin
        rows_ref[:, 2 * p + 1] = im * cos - re * sin
    y_ids = lax.broadcasted_iota(jnp.int32, (CELLS, CELLS), 0).astype(BF16)
    one, zero = jnp.ones((CELLS, CELLS), BF16), jnp.zeros((CELLS, CELLS), BF16)
    y_cells = (cell & (CELLS - 1)).astype(BF16)
    for j in range(LAYERS):
        spot = jnp.where(y_ids == y_cells[j], one, zero)
        values = rows_ref[j].reshape(4 * ROWS, CELLS)
        high = values.astype(BF16)
        low = (values - high.astype(F32)).astype(BF16)
        at_y = lax.dot_general(
            jnp.concatenate([high, low], axis=0), spot, (((1,), (1,)), ((), ())),
            preferred_element_type=F32,
        )
        rows_ref[j] = (at_y[: 4 * ROWS] + at_y[4 * ROWS :]).reshape(4, ROWS, CELLS)
    mix_rows(rows_ref, green_ref, place_ref, places, table_ref, out_ref, spec_ref, kern_ref, mixed_ref)


def x_inverse(rows_ref, table_ref):
    parts = [
        jnp.concatenate(
            [rows_ref[:, 2 * p + c].reshape(WAVES, CELLS) for p in range(POLS)], axis=1
        )
        for c in range(2)
    ]
    waves = jnp.concatenate(parts, axis=0)
    cells = jnp.dot(thrice(table_ref[...], 1), split_cat(waves, 0), preferred_element_type=F32)
    return [
        [cells[c * CELLS : (c + 1) * CELLS, p * CELLS : (p + 1) * CELLS] for c in range(2)]
        for p in range(POLS)
    ]


def residual_kernel(rows_ref, field_ref, station_ref, seen_ref, error_ref, table_ref, total_ref, sent_ref):
    scattered = x_inverse(rows_ref, table_ref)
    cell = station_ref[...]
    ids = lax.broadcasted_iota(jnp.int32, (CELLS, CELLS), 0)
    x_spot = jnp.where(ids == (cell >> 7), 1.0, 0.0).astype(BF16)
    y_spot = ids == (cell & (CELLS - 1))
    sent = []
    for p in range(POLS):
        weight = error_ref[0, p] * error_ref[0, p]
        for c in range(2):
            total = field_ref[0, p, c, 0] + scattered[p][c]
            total_ref[2 * p + c] = total
            turned = total.T
            picked = jnp.zeros((CELLS, CELLS), F32)
            for _ in range(3):
                piece = turned.astype(BF16)
                picked = picked + jnp.dot(piece, x_spot, preferred_element_type=F32)
                turned = turned - piece.astype(F32)
            predicted = jnp.sum(jnp.where(y_spot, picked, 0.0), axis=0, keepdims=True)
            resid = (predicted - seen_ref[0, p, c]) / weight
            sent.append(-resid if c else resid)
    sent.append(cell.astype(F32))
    message = jnp.concatenate(sent, axis=1)
    sent_ref[...] = jnp.broadcast_to(message[None], (LAYERS, 1, 5 * CELLS))


def gradient_kernel(rows_ref, total_ref, table_ref, out_ref):
    adjoint = x_inverse(rows_ref, table_ref)
    term = jnp.zeros((CELLS, CELLS), F32)
    for p in range(POLS):
        term = term + (total_ref[2 * p] * adjoint[p][0] - total_ref[2 * p + 1] * adjoint[p][1])
    out_ref[...] = jnp.broadcast_to(term[None], (RING, CELLS, CELLS))


def call(kernel, out_shape, scratch=(), loose=0, operands=()):
    specs = [pl.BlockSpec(memory_space=pl.ANY)] * loose
    specs += [pl.BlockSpec(memory_space=pltpu.VMEM)] * (len(operands) - loose)
    if isinstance(out_shape, list):
        out_specs = [pl.BlockSpec(memory_space=pltpu.VMEM)] * len(out_shape)
    else:
        out_specs = pl.BlockSpec(memory_space=pltpu.VMEM)
    return pl.pallas_call(
        kernel,
        out_shape=out_shape,
        in_specs=specs,
        out_specs=out_specs,
        scratch_shapes=list(scratch),
        compiler_params=pltpu.CompilerParams(vmem_limit_bytes=VMEM_BYTES),
    )(*operands)


def over_layers(values):
    groups = [[k ^ LEAD for k in range(LAYERS)]]
    return lax.all_to_all(
        values, "layer", split_axis=0, concat_axis=0, tiled=True, axis_index_groups=groups
    )


def sum_over_freq(copies, size):
    rings = [[r + k for k in (2, 1, 0, 3)] for r in range(0, size, RING)]
    lines = [[r + RING * k for k in (2, 1, 0, 3)] for r in range(RING)]
    for by_core in ((rings, lines), (lines, rings)):
        groups = [
            [member * LAYERS + layer for member in group]
            for layer in range(LAYERS)
            for group in by_core[layer % 2]
        ]
        parts = lax.all_to_all(
            copies, ("freq", "layer"), split_axis=0, concat_axis=0, tiled=True, axis_index_groups=groups
        )
        total = (parts[0] + parts[1]) + (parts[2] + parts[3])
        copies = jnp.broadcast_to(total[None], copies.shape)
    return total


def per_device(conductivity, background, green, pair_table, stations, observed, data_error, freqs):
    x_fwd, y_both, x_inv = dft_blocks()
    rows_shape = jax.ShapeDtypeStruct((LAYERS, 4, ROWS, CELLS), F32)
    scratch = (
        pltpu.VMEM((2, LAYERS, 3 * POLS * ROWS, CELLS), F32),
        pltpu.VMEM((2, KERNELS, 3 * ROWS, CELLS), F32),
        pltpu.VMEM((POLS, LAYERS, ROWS, 2 * WAVES), F32),
        pltpu.SMEM(pair_table.shape, jnp.int32),
        pltpu.SemaphoreType.DMA(()),
    )
    rows, places = pl.pallas_call(
        x_forward_kernel,
        out_shape=[rows_shape, jax.ShapeDtypeStruct(pair_table.shape, jnp.int32)],
        in_specs=[pl.BlockSpec(memory_space=pl.ANY)] * 4,
        out_specs=[pl.BlockSpec(memory_space=pltpu.VMEM)] * 2,
        scratch_shapes=[
            pltpu.VMEM(conductivity.shape, F32),
            pltpu.VMEM(background.shape, F32),
            pltpu.VMEM(x_fwd.shape, BF16),
            pltpu.VMEM(pair_table.shape, jnp.int32),
            pltpu.SemaphoreType.DMA((4,)),
        ],
        compiler_params=pltpu.CompilerParams(vmem_limit_bytes=FIRST_BYTES),
    )(conductivity, background, x_fwd, pair_table)
    back = call(
        mix_kernel, rows_shape, scratch, 1,
        (places, over_layers(rows), green, y_both),
    )
    total, sent = call(
        residual_kernel,
        [
            jax.ShapeDtypeStruct((4, CELLS, CELLS), F32),
            jax.ShapeDtypeStruct((LAYERS, 1, 5 * CELLS), F32),
        ],
        operands=(over_layers(back), background, stations, observed, data_error, x_inv),
    )
    back = call(
        adjoint_mix_kernel, rows_shape,
        (pltpu.VMEM((LAYERS, 4, ROWS, CELLS), F32),) + scratch, 1,
        (places, over_layers(sent), green, y_both),
    )
    copies = call(
        gradient_kernel,
        jax.ShapeDtypeStruct((RING, CELLS, CELLS), F32),
        operands=(over_layers(back), total, x_inv),
    )
    return sum_over_freq(copies, freqs)[None]


def solution(mesh):
    in_specs = (
        P("layer", None, None),
        P("freq", None, None, "layer", None, None),
        P("freq", None, None, "layer", None),
        P(),
        P("layer", None),
        P("freq", None, None, "layer", None),
        P("freq", None, "layer", None),
    )
    return jax.shard_map(
        functools.partial(per_device, freqs=mesh.shape["freq"]),
        mesh=mesh, in_specs=in_specs, out_specs=P("layer", None, None), check_vma=False,
    )
```

```python
import functools
import math

import jax
import jax.numpy as jnp
import ml_dtypes
import numpy as np
from jax import lax
from jax.experimental import pallas as pl
from jax.experimental.pallas import tpu as pltpu
from jax.sharding import PartitionSpec as P

CELLS = 128
WAVES = 256
LAYERS = 32
ROWS = 8
KERNELS = 32
KERN_ROWS = 6 * ROWS
POLS = 2
GROUP = 2
STEP = 16
RING = 4
LEAD = 27
SIN_PI = (0.0776576603, -0.5982912856, 2.5500775232, -5.1677100835, 3.1415926401)
F32 = jnp.float32
BF16 = jnp.bfloat16
VMEM_BYTES = 40 * 1024 * 1024
FIRST_BYTES = 60 * 1024 * 1024


def halves(table):
    high = table.astype(ml_dtypes.bfloat16)
    low = (table - high.astype(np.float64)).astype(ml_dtypes.bfloat16)
    return high, low


def dft_blocks():
    waves = np.arange(WAVES)[:, None]
    cells = np.arange(CELLS)[None, :]
    angles = (waves * cells % WAVES) * (2.0 * math.pi / WAVES)
    cos, sin = np.cos(angles), np.sin(angles)
    parts = np.arange(WAVES).reshape(LAYERS, ROWS)[np.arange(LAYERS) ^ LEAD].reshape(-1)
    x_fwd = np.concatenate([cos, sin], axis=1)[parts]
    y_fwd = np.block([[cos.T, -sin.T], [sin.T, cos.T]])
    y_inv = np.block([[cos, sin], [-sin, cos]]) / WAVES
    x_inv = np.block([[cos[parts].T, -sin[parts].T], [sin[parts].T, cos[parts].T]]) / WAVES
    y_both = np.concatenate(
        [np.concatenate(halves(y_fwd), axis=0), np.concatenate(halves(y_inv), axis=1)], axis=0
    )
    return np.concatenate(halves(x_fwd), axis=1), y_both, np.concatenate(halves(x_inv), axis=1)


def thrice(table, axis):
    high, low = jnp.split(table, 2, axis=axis)
    return jnp.concatenate([high, high, low], axis=axis)


def split_cat(values, axis):
    high = values.astype(BF16)
    low = (values - high.astype(F32)).astype(BF16)
    return jnp.concatenate([high, low, high], axis=axis)


def x_forward_kernel(
    cond_hbm, field_hbm, table_hbm, pair_hbm,
    out_ref, place_ref, cond_ref, field_ref, table_ref, pair_ref, sems,
):
    moves = ((field_hbm, field_ref), (cond_hbm, cond_ref), (table_hbm, table_ref), (pair_hbm, pair_ref))
    copies = [
        pltpu.make_async_copy(source, target, sems.at[n])
        for n, (source, target) in enumerate(moves)
    ]
    for copy in copies:
        copy.start()
    copies[0].wait()
    copies[1].wait()
    cond = cond_ref[0]
    high, low = [], []
    for c in range(2):
        part = jnp.concatenate([cond * field_ref[0, p, c, 0] for p in range(POLS)], axis=1)
        high.append(part.astype(BF16))
        low.append((part - high[c].astype(F32)).astype(BF16))
    stacks = [
        jnp.concatenate([jnp.concatenate([part[0], part[1]], axis=1), jnp.concatenate([part[1], -part[0]], axis=1)], axis=0)
        for part in (high, low)
    ]
    cells = jnp.concatenate([stacks[0], stacks[1], stacks[0]], axis=0)
    copies[3].wait()
    place_ref[...] = pair_ref[...] * KERN_ROWS
    copies[2].wait()
    rows = jnp.dot(thrice(table_ref[...], 1), cells, preferred_element_type=F32)
    for c in range(2):
        for p in range(POLS):
            at = (c * POLS + p) * CELLS
            out_ref[:, 2 * p + c] = rows[:, at : at + CELLS].reshape(LAYERS, ROWS, CELLS)


def mix_rows(rows_ref, green_ref, place_ref, places, table_ref, out_ref, spec_ref, kern_ref, mixed_ref):
    forward = thrice(table_ref[: 2 * WAVES], 0)
    for p in range(POLS):
        flat = [rows_ref[:, 2 * p + c].reshape(LAYERS * ROWS, CELLS) for c in range(2)]
        both = jnp.concatenate(flat, axis=1)
        spec = jnp.dot(split_cat(both, 1), forward, preferred_element_type=F32)
        if p == 0:
            for h in range(2):
                g_re = green_ref[0, 0, :, :, h * CELLS : (h + 1) * CELLS]
                g_im = green_ref[0, 1, :, :, h * CELLS : (h + 1) * CELLS]
                for k, value in enumerate((g_re + g_im, g_re, g_im)):
                    at = (3 * h + k) * ROWS
                    kern_ref[:, at : at + ROWS] = value
        for h in range(2):
            re = spec[:, h * CELLS : (h + 1) * CELLS].reshape(LAYERS, ROWS, CELLS)
            im = spec[:, WAVES + h * CELLS : WAVES + (h + 1) * CELLS].reshape(LAYERS, ROWS, CELLS)
            for k, value in enumerate((re, im - re, re + im)):
                at = ((h * POLS + p) * 3 + k) * ROWS
                spec_ref[:, at : at + ROWS] = value

    places.wait()
    kern = kern_ref.reshape(KERNELS * KERN_ROWS, CELLS)
    terms = [(r, h, p, k) for r in range(GROUP) for h in range(2) for k in range(3) for p in range(POLS)]

    def one_group(group, carry):
        first = group * GROUP
        first_layer = (group ^ (LEAD // GROUP)) * GROUP

        def some_sources(chunk, sums):
            sums = dict(zip(terms, sums))
            for s in range(STEP):
                j = chunk * STEP + s
                src = [spec_ref[j, k * ROWS : (k + 1) * ROWS] for k in range(6 * POLS)]
                layer = (chunk ^ (LEAD // STEP)) * STEP + (s ^ (LEAD % STEP))
                for r in range(GROUP):
                    place = place_ref[first_layer + (r ^ (LEAD % GROUP)), layer]
                    for h in range(2):
                        for k in range(3):
                            row = pl.multiple_of(place + (3 * h + k) * ROWS, ROWS)
                            factor = kern[pl.ds(row, ROWS), :]
                            for p in range(POLS):
                                sums[r, h, p, k] = sums[r, h, p, k] + factor * src[(h * POLS + p) * 3 + k]
            return tuple(sums[term] for term in terms)

        zero = jnp.zeros((ROWS, CELLS), F32)
        sums = lax.fori_loop(0, LAYERS // STEP, some_sources, (zero,) * len(terms))
        sums = dict(zip(terms, sums))
        for r in range(GROUP):
            for h in range(2):
                for p in range(POLS):
                    one, two, three = (sums[r, h, p, k] for k in range(3))
                    mixed_ref[p, first + r, :, h * CELLS : (h + 1) * CELLS] = one - three
                    mixed_ref[p, first + r, :, WAVES + h * CELLS : WAVES + (h + 1) * CELLS] = one + two
        return carry

    lax.fori_loop(0, LAYERS // GROUP, one_group, 0)

    high, low = table_ref[2 * WAVES :, :WAVES], table_ref[2 * WAVES :, WAVES:]
    inverse = jnp.concatenate([high, high, low], axis=0)
    for p in range(POLS):
        mixed = mixed_ref[p].reshape(LAYERS * ROWS, 2 * WAVES)
        back = jnp.dot(split_cat(mixed, 1), inverse, preferred_element_type=F32)
        for c in range(2):
            out_ref[:, 2 * p + c] = back[:, c * CELLS : (c + 1) * CELLS].reshape(LAYERS, ROWS, CELLS)


def mix_kernel(
    place_any, rows_ref, green_ref, table_ref, out_ref, spec_ref, kern_ref, mixed_ref, place_ref, sem
):
    places = pltpu.make_async_copy(place_any, place_ref, sem)
    places.start()
    mix_rows(rows_ref, green_ref, place_ref, places, table_ref, out_ref, spec_ref, kern_ref, mixed_ref)


def sin_pi(v):
    square = v * v
    total = jnp.full_like(v, SIN_PI[0])
    for factor in SIN_PI[1:]:
        total = total * square + factor
    return total * v


def adjoint_mix_kernel(
    place_any, sent_ref, green_ref, table_ref,
    out_ref, rows_ref, spec_ref, kern_ref, mixed_ref, place_ref, sem,
):
    places = pltpu.make_async_copy(place_any, place_ref, sem)
    places.start()
    sent = [sent_ref[:, :, k * CELLS : (k + 1) * CELLS] for k in range(5)]
    cell = sent[4].astype(jnp.int32)
    x_cell = cell >> 7
    wave = lax.axis_index("layer") * ROWS + lax.broadcasted_iota(jnp.int32, (LAYERS, ROWS, CELLS), 1)
    turn = (wave * x_cell) & (WAVES - 1)
    u = (turn.astype(F32) - WAVES / 2) * (2.0 / WAVES)
    size = jnp.abs(u)
    cos = -sin_pi(0.5 - size)
    sin = sin_pi(jnp.minimum(size, 1.0 - size))
    sin = jnp.where(u < 0, sin, -sin)
    for p in range(POLS):
        re, im = sent[2 * p], sent[2 * p + 1]
        rows_ref[:, 2 * p] = re * cos + im * sin
        rows_ref[:, 2 * p + 1] = im * cos - re * sin
    y_ids = lax.broadcasted_iota(jnp.int32, (CELLS, CELLS), 0).astype(BF16)
    one, zero = jnp.ones((CELLS, CELLS), BF16), jnp.zeros((CELLS, CELLS), BF16)
    y_cells = (cell & (CELLS - 1)).astype(BF16)
    for j in range(LAYERS):
        spot = jnp.where(y_ids == y_cells[j], one, zero)
        values = rows_ref[j].reshape(4 * ROWS, CELLS)
        high = values.astype(BF16)
        low = (values - high.astype(F32)).astype(BF16)
        at_y = lax.dot_general(
            jnp.concatenate([high, low], axis=0), spot, (((1,), (1,)), ((), ())),
            preferred_element_type=F32,
        )
        rows_ref[j] = (at_y[: 4 * ROWS] + at_y[4 * ROWS :]).reshape(4, ROWS, CELLS)
    mix_rows(rows_ref, green_ref, place_ref, places, table_ref, out_ref, spec_ref, kern_ref, mixed_ref)


def x_inverse(rows_ref, table_ref):
    parts = [
        jnp.concatenate(
            [rows_ref[:, 2 * p + c].reshape(WAVES, CELLS) for p in range(POLS)], axis=1
        )
        for c in range(2)
    ]
    waves = jnp.concatenate(parts, axis=0)
    cells = jnp.dot(thrice(table_ref[...], 1), split_cat(waves, 0), preferred_element_type=F32)
    return [
        [cells[c * CELLS : (c + 1) * CELLS, p * CELLS : (p + 1) * CELLS] for c in range(2)]
        for p in range(POLS)
    ]


def residual_kernel(rows_ref, field_ref, station_ref, seen_ref, error_ref, table_ref, total_ref, sent_ref):
    scattered = x_inverse(rows_ref, table_ref)
    cell = station_ref[...]
    ids = lax.broadcasted_iota(jnp.int32, (CELLS, CELLS), 0)
    x_spot = jnp.where(ids == (cell >> 7), 1.0, 0.0).astype(BF16)
    y_spot = ids == (cell & (CELLS - 1))
    sent = []
    for p in range(POLS):
        weight = error_ref[0, p] * error_ref[0, p]
        for c in range(2):
            total = field_ref[0, p, c, 0] + scattered[p][c]
            total_ref[2 * p + c] = total
            turned = total.T
            picked = jnp.zeros((CELLS, CELLS), F32)
            for _ in range(3):
                piece = turned.astype(BF16)
                picked = picked + jnp.dot(piece, x_spot, preferred_element_type=F32)
                turned = turned - piece.astype(F32)
            predicted = jnp.sum(jnp.where(y_spot, picked, 0.0), axis=0, keepdims=True)
            resid = (predicted - seen_ref[0, p, c]) / weight
            sent.append(-resid if c else resid)
    sent.append(cell.astype(F32))
    message = jnp.concatenate(sent, axis=1)
    sent_ref[...] = jnp.broadcast_to(message[None], (LAYERS, 1, 5 * CELLS))


def gradient_kernel(rows_ref, total_ref, table_ref, out_ref):
    adjoint = x_inverse(rows_ref, table_ref)
    term = jnp.zeros((CELLS, CELLS), F32)
    for p in range(POLS):
        term = term + (total_ref[2 * p] * adjoint[p][0] - total_ref[2 * p + 1] * adjoint[p][1])
    out_ref[...] = jnp.broadcast_to(term[None], (RING, CELLS, CELLS))


def call(kernel, out_shape, scratch=(), loose=0, operands=()):
    specs = [pl.BlockSpec(memory_space=pl.ANY)] * loose
    specs += [pl.BlockSpec(memory_space=pltpu.VMEM)] * (len(operands) - loose)
    if isinstance(out_shape, list):
        out_specs = [pl.BlockSpec(memory_space=pltpu.VMEM)] * len(out_shape)
    else:
        out_specs = pl.BlockSpec(memory_space=pltpu.VMEM)
    return pl.pallas_call(
        kernel,
        out_shape=out_shape,
        in_specs=specs,
        out_specs=out_specs,
        scratch_shapes=list(scratch),
        compiler_params=pltpu.CompilerParams(vmem_limit_bytes=VMEM_BYTES),
    )(*operands)


def over_layers(values):
    groups = [[k ^ LEAD for k in range(LAYERS)]]
    return lax.all_to_all(
        values, "layer", split_axis=0, concat_axis=0, tiled=True, axis_index_groups=groups
    )


def sum_over_freq(copies, size):
    rings = [[r + k for k in (2, 1, 0, 3)] for r in range(0, size, RING)]
    lines = [[r + RING * k for k in (2, 1, 0, 3)] for r in range(RING)]
    for by_core in ((rings, lines), (lines, rings)):
        groups = [
            [member * LAYERS + layer for member in group]
            for layer in range(LAYERS)
            for group in by_core[layer % 2]
        ]
        parts = lax.all_to_all(
            copies, ("freq", "layer"), split_axis=0, concat_axis=0, tiled=True, axis_index_groups=groups
        )
        total = (parts[0] + parts[1]) + (parts[2] + parts[3])
        copies = jnp.broadcast_to(total[None], copies.shape)
    return total


def per_device(conductivity, background, green, pair_table, stations, observed, data_error, freqs):
    x_fwd, y_both, x_inv = dft_blocks()
    rows_shape = jax.ShapeDtypeStruct((LAYERS, 4, ROWS, CELLS), F32)
    scratch = (
        pltpu.VMEM((LAYERS, 6 * POLS * ROWS, CELLS), F32),
        pltpu.VMEM((KERNELS, KERN_ROWS, CELLS), F32),
        pltpu.VMEM((POLS, LAYERS, ROWS, 2 * WAVES), F32),
        pltpu.SMEM(pair_table.shape, jnp.int32),
        pltpu.SemaphoreType.DMA(()),
    )
    rows, places = pl.pallas_call(
        x_forward_kernel,
        out_shape=[rows_shape, jax.ShapeDtypeStruct(pair_table.shape, jnp.int32)],
        in_specs=[pl.BlockSpec(memory_space=pl.ANY)] * 4,
        out_specs=[pl.BlockSpec(memory_space=pltpu.VMEM)] * 2,
        scratch_shapes=[
            pltpu.VMEM(conductivity.shape, F32),
            pltpu.VMEM(background.shape, F32),
            pltpu.VMEM(x_fwd.shape, BF16),
            pltpu.VMEM(pair_table.shape, jnp.int32),
            pltpu.SemaphoreType.DMA((4,)),
        ],
        compiler_params=pltpu.CompilerParams(vmem_limit_bytes=FIRST_BYTES),
    )(conductivity, background, x_fwd, pair_table)
    back = call(
        mix_kernel, rows_shape, scratch, 1,
        (places, over_layers(rows), green, y_both),
    )
    total, sent = call(
        residual_kernel,
        [
            jax.ShapeDtypeStruct((4, CELLS, CELLS), F32),
            jax.ShapeDtypeStruct((LAYERS, 1, 5 * CELLS), F32),
        ],
        operands=(over_layers(back), background, stations, observed, data_error, x_inv),
    )
    back = call(
        adjoint_mix_kernel, rows_shape,
        (pltpu.VMEM((LAYERS, 4, ROWS, CELLS), F32),) + scratch, 1,
        (places, over_layers(sent), green, y_both),
    )
    copies = call(
        gradient_kernel,
        jax.ShapeDtypeStruct((RING, CELLS, CELLS), F32),
        operands=(over_layers(back), total, x_inv),
    )
    return sum_over_freq(copies, freqs)[None]


def solution(mesh):
    in_specs = (
        P("layer", None, None),
        P("freq", None, None, "layer", None, None),
        P("freq", None, None, "layer", None),
        P(),
        P("layer", None),
        P("freq", None, None, "layer", None),
        P("freq", None, "layer", None),
    )
    return jax.shard_map(
        functools.partial(per_device, freqs=mesh.shape["freq"]),
        mesh=mesh, in_specs=in_specs, out_specs=P("layer", None, None), check_vma=False,
    )
```
